32 devices in a mesh: seq: 4 (over z), dp: 8 (over y, x, core).
Axes of the slice: x: 2, y: 2, z: 4, core: 2. Of those that a mesh axis runs over, the one named last changes fastest.
Arguments:
- queries: bfloat16 [8, 512, 1024], P('dp', 'seq'), may hold values from -16 to 16
- saved_output: bfloat16 [8, 512, 1024], P('dp', 'seq'), may hold values from -6 to 6
- grad_out: bfloat16 [8, 512, 1024], P('dp', 'seq'), may hold values from -6 to 6
- tile_kv: bfloat16 [16, 1601, 512], P('dp', None, 'seq'), may hold values from -16 to 16
- tile_count: int32 [8], replicated, may hold values from 1 to 4, 12 in all
- owner_perm: int32 [8], replicated, may hold values from 0 to 7, each once
- text_len: int32 [8], P('dp'), may hold values from 128 to 512
Outputs:
- grad_queries: bfloat16 [8, 512, 1024], P('dp', 'seq')
- grad_tile_kv: bfloat16 [16, 1601, 512], P('dp', None, 'seq')
The draws below stay inside these ranges and needn't reach their ends.
Inputs may be any that keep to these rules, and one draw needn't show every extreme that they name: `tile_count`: the counts sum to 12, and some sample has 4 tiles.
All inputs are finite; a program needn't handle non-finite values.
Results may differ from the reference program's by a relative error of at most 0.0061.
Values may be sent and summed in bfloat16 or wider, within the bound.
No kernel may reach another device: no remote copies, remote signals or barrier semaphores. Data moves between devices by JAX's collectives and lax.ppermute only.
A program may use at most 128 MiB of HBM per device.

```python
import math
import jax
import jax.numpy as jnp
import numpy as np
from jax import lax

HEAD_DIM = 128
TILE_ROWS = 1601
MAX_TILES = 4
TEXT = 512
HEADS = 8
KV_HEADS = 2
SAMPLES = 8
OWNER_SLOTS = 16
TILES_USED = 12


def draw_queries(key, part):
    key = jax.random.fold_in(key, 11)
    full_shape = (SAMPLES, TEXT, HEADS * HEAD_DIM)
    return jnp.clip(jax.random.normal(key, full_shape, jnp.float32), -6.0, 6.0).astype(jnp.bfloat16)


def draw_tile_kv(key, part):
    key = jax.random.fold_in(key, 23)
    full_shape = (OWNER_SLOTS, TILE_ROWS, 2 * KV_HEADS * HEAD_DIM)
    return jnp.clip(jax.random.normal(key, full_shape, jnp.float32), -6.0, 6.0).astype(jnp.bfloat16)


def touch_ends(entries, key, smallest, high):
    place = [jax.random.randint(jax.random.fold_in(key, axis), (), 0, length) for axis, length in enumerate(entries.shape)]
    longest = entries.shape.index(max(entries.shape))
    beside = place[:longest] + [(place[longest] + 1) % entries.shape[longest]] + place[longest + 1:]
    return entries.at[tuple(place)].set(smallest).at[tuple(beside)].set(high)


def level_of(stream_key, dims, cuts, least, largest):
    loudness = 1.0
    for axis_at, parts in cuts:
        steps = jax.random.uniform(jax.random.fold_in(jax.random.fold_in(stream_key, 6), axis_at), (parts,), jnp.float32, least / len(cuts), largest / len(cuts))
        loudness = loudness * jnp.repeat(jnp.exp(steps), dims[axis_at] // parts).reshape((-1,) + (1,) * (len(dims) - 1 - axis_at))
    return loudness


def split_up(count, total, most, slope):
    loads = [(1 << 20) // math.isqrt(rank ** slope) + 1 for rank in range(2, count + 1)]
    spare, given = total - most - (count - 1), [1] * (count - 1)
    while spare > 0:
        free = [i for i in range(count - 1) if given[i] < most]
        pool, left = sum([loads[i] for i in free]), spare
        for i in free:
            extra = min(most - given[i], max(1, left * loads[i] // pool), spare)
            given[i] = given[i] + extra
            spare = spare - extra
    return np.array([most] + given)


def uneven(own_key, number_of, total, reach, lean):
    if number_of == 2:
        one = jax.random.randint(own_key, (), max(1, total - reach), min(reach, total - 1) + 1)
        return jnp.stack([one, total - one])
    sizes = jnp.asarray(split_up(number_of, total, reach, lean), jnp.int32)
    pairs = (number_of - 1) // 2
    donor, taker = sizes[1:1 + 2 * pairs:2], sizes[2:2 + 2 * pairs:2]
    margin = jnp.minimum(donor - 1, reach - taker)
    shifted = jax.random.randint(jax.random.fold_in(own_key, 1), (pairs,), 0, 1 << 20) % (margin + 1)
    sizes = sizes.at[1:1 + 2 * pairs:2].set(donor - shifted).at[2:2 + 2 * pairs:2].set(taker + shifted)
    return sizes[jax.random.permutation(jax.random.fold_in(own_key, 2), number_of)]


def scatter_about(rng, extent, spread, limit, cuts=(), held_as=jnp.bfloat16):
    result = spread * jax.random.normal(rng, extent, jnp.float32)
    if cuts:
        result = result * level_of(rng, extent, cuts, -0.22, 0.18)
    return jnp.clip(result, -limit, limit).astype(held_as)


def setup_inputs(seed: int = 0) -> dict:
    seeds = jax.random.split(jax.random.key(seed), 8)
    queries = draw_queries(jax.random.fold_in(seeds[7], 71), 0)
    saved_output = scatter_about(seeds[1], (SAMPLES, TEXT, HEADS * HEAD_DIM), 1.0, 6.0, ((0, 8), (1, 4)))
    grad_out = scatter_about(seeds[2], (SAMPLES, TEXT, HEADS * HEAD_DIM), 1.0, 6.0, ((0, 8), (1, 4)))
    tile_kv = draw_tile_kv(jax.random.fold_in(seeds[7], 71), 0)
    tile_count = uneven(seeds[4], SAMPLES, TILES_USED, MAX_TILES, 2).astype(jnp.int32)
    owner_perm = jax.random.permutation(seeds[5], SAMPLES).astype(jnp.int32)
    text_len = touch_ends(jax.random.randint(seeds[6], (SAMPLES,), TEXT // 4, TEXT + 1), jax.random.fold_in(seeds[6], 1), TEXT // 4, TEXT).astype(jnp.int32)
    return {"queries": queries, "saved_output": saved_output, "grad_out": grad_out, "tile_kv": tile_kv, "tile_count": tile_count, "owner_perm": owner_perm, "text_len": text_len}


def tile_places(tile_count, owner_perm, slots_owner):
    samples = tile_count.shape[0]
    offsets = jnp.cumsum(tile_count) - tile_count
    within = jnp.arange(MAX_TILES, dtype=jnp.int32)
    slot_valid = within[None, :] < tile_count[:, None]
    places = offsets[:, None] + jnp.where(slot_valid, within[None, :], 0)
    owners = owner_perm[places % samples]
    return ((owners * slots_owner + places // samples).astype(jnp.int32), slot_valid)

def head_pair(query_pair, grad_pair, delta_pair, key_rows, value_rows, key_mask, score_scale):
    query_wide = query_pair.astype(jnp.float32)
    grad_wide = grad_pair.astype(jnp.float32)
    key_wide = key_rows.astype(jnp.float32)
    value_wide = value_rows.astype(jnp.float32)
    scores = jnp.einsum('thd,rd->htr', query_wide, key_wide) * score_scale
    scores = jnp.where(key_mask[None, None, :], scores, -jnp.inf)
    row_peak = lax.optimization_barrier(jnp.max(scores, axis=2, keepdims=True))
    weights = jnp.exp(scores - row_peak)
    attention = weights / lax.optimization_barrier(jnp.sum(weights, axis=2, keepdims=True))
    attention_half = lax.optimization_barrier(attention.astype(jnp.bfloat16)).astype(jnp.float32)
    grad_attention = jnp.einsum('thd,rd->htr', grad_wide, value_wide)
    delta_wide = jnp.transpose(delta_pair.astype(jnp.float32))[:, :, None]
    grad_scores = attention * (grad_attention - delta_wide)
    scores_half = lax.optimization_barrier(grad_scores.astype(jnp.bfloat16)).astype(jnp.float32)
    grad_query = jnp.einsum('htr,rd->thd', scores_half, key_wide) * score_scale
    grad_key = jnp.einsum('htr,thd->rd', scores_half, query_wide) * score_scale
    grad_value = jnp.einsum('htr,thd->rd', attention_half, grad_wide)
    return (grad_query, grad_key, grad_value)

def pair_sum(first_part, second_part):
    first_half = lax.optimization_barrier(first_part.astype(jnp.bfloat16)).astype(jnp.float32)
    second_half = lax.optimization_barrier(second_part.astype(jnp.bfloat16)).astype(jnp.float32)
    return (first_half + second_half).astype(jnp.bfloat16)

def reference(queries, saved_output, grad_out, tile_kv, tile_count, owner_perm, text_len):
    samples, text_rows, feature_width = queries.shape
    head_count = feature_width // HEAD_DIM
    kv_count = head_count // 4
    tile_rows = tile_kv.shape[1]
    kv_width = tile_kv.shape[2]
    score_scale = 1.0 / math.sqrt(HEAD_DIM)
    position = jnp.arange(text_rows, dtype=jnp.int32)
    keep_rows = position[None, :] < text_len[:, None]
    masked_grad = jnp.where(keep_rows[:, :, None], grad_out, jnp.zeros_like(grad_out))
    products = masked_grad.astype(jnp.float32) * saved_output.astype(jnp.float32)
    row_delta = lax.optimization_barrier(jnp.sum(products.reshape(samples, text_rows, head_count, HEAD_DIM), axis=3)).astype(jnp.bfloat16)
    global_slot, slot_valid = tile_places(tile_count, owner_perm, tile_kv.shape[0] // samples)

    def one_sample(inputs):
        query_rows, grad_rows, delta_rows, slot_ids, slot_live = inputs
        tile_block = jnp.take(tile_kv, slot_ids, axis=0)
        tile_block = tile_block.reshape(MAX_TILES * tile_rows, kv_count, 2, HEAD_DIM)
        key_mask = jnp.repeat(slot_live, tile_rows)
        query_view = query_rows.reshape(text_rows, kv_count, 2, 2, HEAD_DIM)
        grad_view = grad_rows.reshape(text_rows, kv_count, 2, 2, HEAD_DIM)
        delta_view = delta_rows.reshape(text_rows, kv_count, 2, 2)

        def one_head(head_index):
            kv_select = lax.dynamic_index_in_dim(tile_block, head_index, 1, keepdims=False)
            query_select = lax.dynamic_index_in_dim(query_view, head_index, 1, keepdims=False)
            grad_select = lax.dynamic_index_in_dim(grad_view, head_index, 1, keepdims=False)
            delta_select = lax.dynamic_index_in_dim(delta_view, head_index, 1, keepdims=False)
            results = []
            for half_index in range(2):
                results.append(head_pair(query_select[:, half_index], grad_select[:, half_index], delta_select[:, half_index], kv_select[:, 0], kv_select[:, 1], key_mask, score_scale))
            grad_query = jnp.stack([results[0][0], results[1][0]], axis=1)
            grad_key = pair_sum(results[0][1], results[1][1])
            grad_value = pair_sum(results[0][2], results[1][2])
            return (grad_query, jnp.stack([grad_key, grad_value], axis=1))
        grad_query, grad_kv = lax.map(one_head, jnp.arange(kv_count, dtype=jnp.int32))
        grad_query = jnp.transpose(grad_query, (1, 0, 2, 3, 4)).reshape(text_rows, feature_width)
        grad_kv = jnp.transpose(grad_kv, (1, 0, 2, 3)).reshape(MAX_TILES, tile_rows, kv_width)
        grad_kv = jnp.where(slot_live[:, None, None], grad_kv, jnp.zeros_like(grad_kv))
        return (grad_query.astype(jnp.bfloat16), grad_kv)
    grad_queries, slot_grads = lax.map(one_sample, (queries, masked_grad, row_delta, global_slot, slot_valid))
    flat_grads = slot_grads.reshape(samples * MAX_TILES, tile_rows, kv_width).astype(jnp.float32)
    grad_tiles = jnp.zeros(tile_kv.shape, jnp.float32).at[global_slot.reshape(-1)].add(flat_grads)
    return (grad_queries, grad_tiles.astype(jnp.bfloat16))
```

```python
import functools
import math

import jax
import jax.numpy as jnp
from jax import lax
from jax.experimental import pallas as pl
from jax.experimental.pallas import tpu as pltpu
from jax.sharding import PartitionSpec as P

HEAD_DIM = 128
MAX_TILES = 4
KEY_ROWS = 256
TEXT_CHUNKS = 4
DELTA_ROWS = 16
SCALE = 1.0 / math.sqrt(HEAD_DIM)
SCALE_LOG2 = SCALE / math.log(2.0)
BF16 = jnp.bfloat16
F32 = jnp.float32

SMEM = pl.BlockSpec(memory_space=pltpu.SMEM)
VMEM = pl.BlockSpec(memory_space=pltpu.VMEM)
ANY = pl.BlockSpec(memory_space=pl.ANY)


def exchange(block, axis, distance):
    count = lax.axis_size(axis)
    return lax.ppermute(block, axis, [(i, i ^ distance) for i in range(count)])


def call(kernel, out_shape, in_specs, scratch, args, out_specs=None, megabytes=16, flops=0, moved=0):
    many = isinstance(out_shape, (list, tuple))
    if out_specs is None:
        out_specs = [VMEM] * len(out_shape) if many else VMEM
    return pl.pallas_call(
        kernel,
        out_shape=out_shape,
        in_specs=in_specs,
        out_specs=out_specs,
        scratch_shapes=scratch,
        compiler_params=pltpu.CompilerParams(vmem_limit_bytes=megabytes << 20),
        cost_estimate=pl.CostEstimate(flops=flops, bytes_accessed=moved, transcendentals=0),
    )(*args)


def place_of(perm_ref, owner, owners):
    first = jnp.int32(0)
    for index in range(owners):
        first = first + jnp.where(perm_ref[index] == owner, index, 0)
    return first


def sample_at(count_ref, place, samples):
    end, sample, start = jnp.int32(0), jnp.int32(0), jnp.int32(0)
    for index in range(samples):
        end = end + count_ref[index]
        passed = place >= end
        sample = sample + passed.astype(jnp.int32)
        start = jnp.where(passed, end, start)
    return sample, start


def pack_kernel(groups, heads, who, length, q_ref, o_ref, g_ref, *outs):
    rows = q_ref.shape[0]
    seq = who[0]
    position = seq * rows + lax.broadcasted_iota(jnp.int32, (rows, HEAD_DIM), 0)
    keep = position < length[0]
    half = heads // 2
    for j in range(groups):
        q_out, g_out = outs[j], outs[groups + j]
        for h in range(heads):
            start = pl.multiple_of(((seq ^ j) * heads + h) * HEAD_DIM, HEAD_DIM)
            columns = pl.ds(start, HEAD_DIM)
            q_out[h // half, h % half] = q_ref[:, columns]
            grad = jnp.where(keep, g_ref[:, columns].astype(F32), 0.0)
            product = grad * o_ref[:, columns].astype(F32)
            delta = jnp.sum(jnp.transpose(product), axis=0, keepdims=True)
            g_out[h // half, h % half, :rows] = grad.astype(BF16)
            g_out[h // half, h % half, rows:] = jnp.broadcast_to(
                delta, (DELTA_ROWS, HEAD_DIM)
            ).astype(BF16)


def fetch(pieces, relative, target, sem):
    for index, piece in enumerate(pieces):
        @pl.when(relative == index)
        def _(piece=piece):
            pltpu.make_async_copy(piece, target, sem).start()


def chunks_of(rows):
    full = rows // KEY_ROWS
    tail = rows - full * KEY_ROWS
    return full, tail, -(-tail // 16) * 16


def dot_nt(a, b):
    return lax.dot_general(a, b, (((1,), (1,)), ((), ())), preferred_element_type=F32)


def dot_nn(a, b):
    return jnp.dot(a, b, preferred_element_type=F32)


def stats_kernel(owners, heads, slots, who, counts, perm, own_kv, partner_kv, *refs):
    q_pieces = (refs[:owners], refs[owners:2 * owners])
    out, q_buf, k_buf, k_tail, q_sem, k_sem = refs[2 * owners:]
    seq, me = who[0], who[1]
    groups = q_buf.shape[2]
    half = heads // 2
    rows = k_buf.shape[1]
    full, tail, tail_pad = chunks_of(rows)
    first = place_of(perm, me, owners)
    samples = [sample_at(counts, first + slot * owners, owners)[0] for slot in range(slots)]
    for slot in range(slots):
        @pl.when(samples[slot] < owners)
        def _(slot=slot):
            @pl.when(seq % 2 == 0)
            def _():
                pltpu.make_async_copy(own_kv.at[slot], k_buf.at[slot], k_sem.at[slot]).start()

            @pl.when(seq % 2 == 1)
            def _():
                pltpu.make_async_copy(partner_kv.at[slot], k_buf.at[slot], k_sem.at[slot]).start()

            for side in range(2):
                fetch(q_pieces[side], samples[slot] ^ me, q_buf.at[slot, side], q_sem.at[slot, side])
    k_tail[...] = jnp.zeros(k_tail.shape, BF16)
    text_chunks = min(TEXT_CHUNKS, groups)
    width = text_chunks * HEAD_DIM

    for slot in range(slots):
        @pl.when(samples[slot] < owners)
        def _(slot=slot):
            pltpu.make_async_copy(own_kv.at[slot], k_buf.at[slot], k_sem.at[slot]).wait()
            for side in range(2):
                pltpu.make_async_copy(q_pieces[side][0], q_buf.at[slot, side], q_sem.at[slot, side]).wait()
            k_tail[:tail] = k_buf[slot, full * KEY_ROWS:]

            def one_block(step, carry):
                head, block = step // (groups // text_chunks), step % (groups // text_chunks)
                query = q_buf[slot, head // half, pl.ds(block * text_chunks, text_chunks), head % half]
                query = query.reshape(width, HEAD_DIM)
                peak = jnp.full((8, width), -jnp.inf, F32)
                mass = jnp.zeros((8, width), F32)
                for chunk in range(full + 1):
                    if chunk < full:
                        scores = dot_nt(k_buf[slot, chunk * KEY_ROWS:(chunk + 1) * KEY_ROWS], query)
                    else:
                        scores = dot_nt(k_tail[...], query)
                        row = lax.broadcasted_iota(jnp.int32, scores.shape, 0)
                        scores = jnp.where(row < tail, scores, -jnp.inf)
                    scores = scores.reshape(-1, 8, width)
                    new_peak = jnp.maximum(peak, jnp.max(scores, axis=0))
                    shift = new_peak * SCALE_LOG2
                    mass = mass * jnp.exp2(peak * SCALE_LOG2 - shift) + jnp.sum(
                        jnp.exp2(scores * SCALE_LOG2 - shift[None]), axis=0
                    )
                    peak = new_peak
                peak = peak * SCALE_LOG2
                top = jnp.max(peak, axis=0, keepdims=True)
                total = jnp.sum(mass * jnp.exp2(peak - top), axis=0, keepdims=True)
                for piece in range(text_chunks):
                    lanes = slice(piece * HEAD_DIM, (piece + 1) * HEAD_DIM)
                    place = block * text_chunks + piece
                    out[slot, 0, head, pl.ds(place, 1)] = top[:, lanes]
                    out[slot, 1, head, pl.ds(place, 1)] = total[:, lanes]
                return carry

            lax.fori_loop(0, heads * (groups // text_chunks), one_block, 0)


def grads_kernel(owners, heads, slots, who, counts, perm, stats, own_kv, partner_kv, *refs):
    q_pieces = (refs[:owners], refs[owners:2 * owners])
    g_pieces = (refs[2 * owners:3 * owners], refs[3 * owners:4 * owners])
    (dq_out, keep_out, send_out, q_buf, g_buf, kv_buf, kv_tail, k_turn, sums, q_sem, g_sem, kv_sem) = refs[4 * owners:]
    seq, me = who[0], who[1]
    parity = seq % 2
    groups = q_buf.shape[2]
    half = heads // 2
    rows = kv_buf.shape[2]
    full, tail, tail_pad = chunks_of(rows)
    first = place_of(perm, me, owners)
    placed = [sample_at(counts, first + slot * owners, owners) for slot in range(slots)]
    for slot in range(slots):
        sample = placed[slot][0]

        @pl.when(sample < owners)
        def _(slot=slot, sample=sample):
            pltpu.make_async_copy(own_kv.at[slot], kv_buf.at[slot, parity], kv_sem.at[slot, 0]).start()
            pltpu.make_async_copy(partner_kv.at[slot], kv_buf.at[slot, 1 - parity], kv_sem.at[slot, 1]).start()
            for side in range(2):
                fetch(q_pieces[side], sample ^ me, q_buf.at[slot, side], q_sem.at[slot, side])
                fetch(g_pieces[side], sample ^ me, g_buf.at[slot, side], g_sem.at[slot, side])
    kv_tail[...] = jnp.zeros(kv_tail.shape, BF16)
    text_chunks = min(TEXT_CHUNKS, groups)
    width = text_chunks * HEAD_DIM
    spans = [(index * KEY_ROWS, KEY_ROWS) for index in range(full)] + [(full * KEY_ROWS, tail_pad)]

    for slot in range(slots):
        sample, start = placed[slot]

        @pl.when(sample >= owners)
        def _(slot=slot):
            keep_out[slot] = jnp.zeros(keep_out.shape[1:], BF16)
            send_out[slot] = jnp.zeros(send_out.shape[1:], BF16)

        @pl.when(sample < owners)
        def _(slot=slot, sample=sample, start=start):
            pltpu.make_async_copy(own_kv.at[slot], kv_buf.at[slot, parity], kv_sem.at[slot, 0]).wait()
            pltpu.make_async_copy(partner_kv.at[slot], kv_buf.at[slot, 1 - parity], kv_sem.at[slot, 1]).wait()
            for side in range(2):
                pltpu.make_async_copy(q_pieces[side][0], q_buf.at[slot, side], q_sem.at[slot, side]).wait()
                pltpu.make_async_copy(g_pieces[side][0], g_buf.at[slot, side], g_sem.at[slot, side]).wait()
            kv_tail[0, :tail] = kv_buf[slot, 0, full * KEY_ROWS:]
            kv_tail[1, :tail] = kv_buf[slot, 1, full * KEY_ROWS:]

            def rows_of(which, index):
                if index < full:
                    return kv_buf[slot, which, index * KEY_ROWS:(index + 1) * KEY_ROWS]
                return kv_tail[which]

            for index, (low, size) in enumerate(spans):
                k_turn[:, low:low + size] = jnp.transpose(rows_of(0, index).astype(F32)).astype(BF16)
            sums[...] = jnp.zeros(sums.shape, F32)
            tiles = counts[jnp.minimum(sample, owners - 1)]

            def normaliser(head, piece):
                found = []
                for index in range(MAX_TILES):
                    live = index < tiles
                    place = jnp.where(live, start + index, start)
                    other = perm[place % owners] ^ me
                    top = stats[other, place // owners, 0, head, pl.ds(piece, 1)]
                    mass = stats[other, place // owners, 1, head, pl.ds(piece, 1)]
                    found.append((jnp.where(live, top, -jnp.inf), jnp.where(live, mass, 0.0)))
                top = functools.reduce(jnp.maximum, [peak for peak, _ in found])
                total = sum(mass * jnp.exp2(peak - top) for peak, mass in found)
                return top + jnp.log2(total)

            def one_block(step, carry):
                head, block = step // (groups // text_chunks), step % (groups // text_chunks)
                side, inner = head // half, head % half
                pieces = pl.ds(block * text_chunks, text_chunks)
                query = q_buf[slot, side, pieces, inner].reshape(width, HEAD_DIM)
                grad = g_buf[slot, side, pieces, inner, :HEAD_DIM].reshape(width, HEAD_DIM)
                delta = jnp.concatenate(
                    [
                        g_buf[slot, side, block * text_chunks + piece, inner, HEAD_DIM:].astype(F32)[:1]
                        for piece in range(text_chunks)
                    ],
                    axis=1,
                )
                level = jnp.concatenate(
                    [normaliser(head, block * text_chunks + piece) for piece in range(text_chunks)], axis=1
                )
                turned = jnp.zeros((HEAD_DIM, width), F32)
                for index, (low, size) in enumerate(spans):
                    scores = dot_nt(rows_of(0, index), query)
                    weights = jnp.exp2(scores * SCALE_LOG2 - level)
                    if index == full:
                        row = lax.broadcasted_iota(jnp.int32, scores.shape, 0)
                        weights = jnp.where(row < tail, weights, 0.0)
                    slope = dot_nt(rows_of(1, index), grad)
                    bent = (weights * (slope - delta)).astype(BF16)
                    turned = turned + dot_nn(k_turn[:, low:low + size], bent)
                    sums[0, low:low + size] += dot_nn(bent, query)
                    sums[1, low:low + size] += dot_nn(weights.astype(BF16), grad)
                result = (jnp.transpose(turned) * SCALE).astype(BF16)
                start_row = pl.multiple_of(block * width, width)
                start_col = pl.multiple_of(head * HEAD_DIM, HEAD_DIM)
                dq_out[slot, pl.ds(start_row, width), pl.ds(start_col, HEAD_DIM)] = result
                return carry

            lax.fori_loop(0, heads * (groups // text_chunks), one_block, 0)
            keep_scale = jnp.where(parity == 0, SCALE, 1.0)
            send_scale = jnp.where(parity == 0, 1.0, SCALE)
            keep_out[slot] = (sums[parity, :rows] * keep_scale).astype(BF16)
            send_out[slot] = (sums[1 - parity, :rows] * send_scale).astype(BF16)


def route_kernel(owners, slots, who, counts, perm, own, other, *outs):
    me = who[1]
    found = []
    for near, source in ((me, own), (me ^ 1, other)):
        first = place_of(perm, near, owners)
        for slot in range(slots):
            found.append((sample_at(counts, first + slot * owners, owners)[0], source, slot))
    block = 128
    for distance, out in enumerate(outs):
        target = me ^ (2 * distance)

        def one(step, carry):
            rows = pl.ds(pl.multiple_of(step * block, block), block)
            total = jnp.zeros((block, out.shape[1]), F32)
            for sample, source, slot in found:
                total = total + jnp.where(sample == target, source[slot, rows].astype(F32), 0.0)
            out[rows] = total.astype(BF16)
            return carry

        lax.fori_loop(0, out.shape[0] // block, one, 0)


def gather_kernel(parts, *refs):
    outs = refs[parts:]
    rows = outs[0].shape[0]
    for piece, out in enumerate(outs):
        span = slice(piece * rows, (piece + 1) * rows)
        out[...] = sum(ref[span].astype(F32) for ref in refs[:parts]).astype(BF16)


def place_kernel(who, *refs):
    out = refs[-1]
    for distance, ref in enumerate(refs[:-1]):
        width = ref.shape[1]
        start = pl.multiple_of((who[0] ^ distance) * width, width)
        out[:, pl.ds(start, width)] = ref[...]


def gather_pieces(block, turn):
    count = lax.axis_size("dp")
    near = {0: block}
    for distance in sorted(range(2, count, 2), key=lambda d: (bin(d).count("1"), d)):
        last = 1 << (distance.bit_length() - 1) if turn == 0 else distance & -distance
        near[distance] = exchange(near[distance ^ last], "dp", last)
    result = [None] * count
    for distance, piece in near.items():
        result[distance] = piece
        result[distance ^ 1] = exchange(piece, "dp", 1)
    return result


def shards(queries, saved_output, grad_out, tile_kv, tile_count, owner_perm, text_len):
    rows_dev, features = queries.shape[1], queries.shape[2]
    groups, owners = lax.axis_size("seq"), lax.axis_size("dp")
    heads = features // HEAD_DIM // groups
    half = heads // 2
    width = heads * HEAD_DIM
    text_rows = groups * rows_dev
    slots, tile_rows = tile_kv.shape[0], tile_kv.shape[1]
    full, tail, tail_pad = chunks_of(tile_rows)
    padded = full * KEY_ROWS + tail_pad
    who = jnp.stack([lax.axis_index("seq"), lax.axis_index("dp")]).astype(jnp.int32)

    q_shape = jax.ShapeDtypeStruct((2, half, rows_dev, HEAD_DIM), BF16)
    g_shape = jax.ShapeDtypeStruct((2, half, rows_dev + DELTA_ROWS, HEAD_DIM), BF16)
    packed = call(
        functools.partial(pack_kernel, groups, heads),
        [q_shape] * groups + [g_shape] * groups,
        [SMEM, SMEM] + [VMEM] * 3,
        [],
        (who, text_len, queries[0], saved_output[0], grad_out[0]),
    )

    def over_seq(pieces):
        got = [pieces[0]] + [exchange(pieces[j], "seq", j) for j in range(1, groups)]
        return [jnp.stack([piece[side] for piece in got]) for side in range(2)]

    q_sides = [gather_pieces(block, side) for side, block in enumerate(over_seq(packed[:groups]))]
    g_sides = [gather_pieces(block, side) for side, block in enumerate(over_seq(packed[groups:]))]
    partner_kv = exchange(tile_kv, "seq", 1)

    stats = call(
        functools.partial(stats_kernel, owners, heads, slots),
        jax.ShapeDtypeStruct((slots, 2, heads, groups, rows_dev), F32),
        [SMEM] * 3 + [ANY] * (2 + 2 * owners),
        [
            pltpu.VMEM((slots, 2, groups, half, rows_dev, HEAD_DIM), BF16),
            pltpu.VMEM((slots, tile_rows, HEAD_DIM), BF16),
            pltpu.VMEM((tail_pad, HEAD_DIM), BF16),
            pltpu.SemaphoreType.DMA((slots, 2)),
            pltpu.SemaphoreType.DMA((slots,)),
        ],
        (who, tile_count, owner_perm, tile_kv, partner_kv, *q_sides[0], *q_sides[1]),
        megabytes=32,
        flops=slots * 2 * width * text_rows * tile_rows,
    )
    pair = jnp.stack([stats, exchange(stats, "dp", 1)])
    all_stats = jnp.concatenate([pair] + [exchange(pair, "dp", d) for d in range(2, owners, 2)])

    kv_shape = jax.ShapeDtypeStruct(tile_kv.shape, BF16)
    grads_q, kv_keep, kv_send = call(
        functools.partial(grads_kernel, owners, heads, slots),
        [jax.ShapeDtypeStruct((slots, text_rows, width), BF16), kv_shape, kv_shape],
        [SMEM] * 3 + [VMEM] + [ANY] * (2 + 4 * owners),
        [
            pltpu.VMEM((slots, 2, groups, half, rows_dev, HEAD_DIM), BF16),
            pltpu.VMEM((slots, 2, groups, half, rows_dev + DELTA_ROWS, HEAD_DIM), BF16),
            pltpu.VMEM((slots, 2, tile_rows, HEAD_DIM), BF16),
            pltpu.VMEM((2, tail_pad, HEAD_DIM), BF16),
            pltpu.VMEM((HEAD_DIM, -(-padded // HEAD_DIM) * HEAD_DIM), BF16),
            pltpu.VMEM((2, padded, HEAD_DIM), F32),
            pltpu.SemaphoreType.DMA((slots, 2)),
            pltpu.SemaphoreType.DMA((slots, 2)),
            pltpu.SemaphoreType.DMA((slots, 2)),
        ],
        (who, tile_count, owner_perm, all_stats, tile_kv, partner_kv, *q_sides[0], *q_sides[1], *g_sides[0], *g_sides[1]),
        megabytes=48,
        flops=slots * 10 * width * text_rows * tile_rows,
    )
    kv_got = exchange(kv_send, "seq", 1)
    grad_tiles = (kv_keep.astype(F32) + kv_got.astype(F32)).astype(BF16)

    sums = call(
        functools.partial(route_kernel, owners, slots),
        [jax.ShapeDtypeStruct((text_rows, width), BF16)] * (owners // 2),
        [SMEM] * 3 + [VMEM] * 2,
        [],
        (who, tile_count, owner_perm, grads_q, exchange(grads_q, "dp", 1)),
        megabytes=32,
    )
    sums = [sums[0]] + [exchange(sums[d], "dp", 2 * d) for d in range(1, owners // 2)]
    cut = call(
        functools.partial(gather_kernel, len(sums)),
        [jax.ShapeDtypeStruct((rows_dev, width), BF16)] * groups,
        [VMEM] * len(sums),
        [],
        sums,
        megabytes=32,
    )
    back = [cut[0]] + [exchange(cut[j], "seq", j) for j in range(1, groups)]
    grad_queries = call(
        place_kernel,
        jax.ShapeDtypeStruct((rows_dev, features), BF16),
        [SMEM] + [VMEM] * groups,
        [],
        (who, *back),
    )
    return (grad_queries[None], grad_tiles)


def solution(mesh):
    placed = (
        P("dp", "seq", None),
        P("dp", "seq", None),
        P("dp", "seq", None),
        P("dp", None, "seq"),
        P(),
        P(),
        P("dp"),
    )
    return jax.shard_map(
        shards,
        mesh=mesh,
        in_specs=placed,
        out_specs=(P("dp", "seq", None), P("dp", None, "seq")),
        check_vma=False,
    )
```

```python
import functools
import math

import jax
import jax.numpy as jnp
from jax import lax
from jax.experimental import pallas as pl
from jax.experimental.pallas import tpu as pltpu
from jax.sharding import PartitionSpec as P

HEAD_DIM = 128
MAX_TILES = 4
KEY_ROWS = 256
TEXT_CHUNKS = 4
DELTA_ROWS = 16
SCALE = 1.0 / math.sqrt(HEAD_DIM)
SCALE_LOG2 = SCALE / math.log(2.0)
BF16 = jnp.bfloat16
F32 = jnp.float32

SMEM = pl.BlockSpec(memory_space=pltpu.SMEM)
VMEM = pl.BlockSpec(memory_space=pltpu.VMEM)
ANY = pl.BlockSpec(memory_space=pl.ANY)


def exchange(block, axis, distance):
    count = lax.axis_size(axis)
    return lax.ppermute(block, axis, [(i, i ^ distance) for i in range(count)])


def call(kernel, out_shape, in_specs, scratch, args, out_specs=None, grid=(), megabytes=16, flops=0, moved=0):
    many = isinstance(out_shape, (list, tuple))
    if out_specs is None:
        out_specs = [VMEM] * len(out_shape) if many else VMEM
    return pl.pallas_call(
        kernel,
        out_shape=out_shape,
        in_specs=in_specs,
        out_specs=out_specs,
        grid=grid,
        scratch_shapes=scratch,
        compiler_params=pltpu.CompilerParams(vmem_limit_bytes=megabytes << 20),
        cost_estimate=pl.CostEstimate(flops=flops, bytes_accessed=moved, transcendentals=0),
    )(*args)


def place_of(perm_ref, owner, owners):
    first = jnp.int32(0)
    for index in range(owners):
        first = first + jnp.where(perm_ref[index] == owner, index, 0)
    return first


def sample_at(count_ref, place, samples):
    end, sample, start = jnp.int32(0), jnp.int32(0), jnp.int32(0)
    for index in range(samples):
        end = end + count_ref[index]
        passed = place >= end
        sample = sample + passed.astype(jnp.int32)
        start = jnp.where(passed, end, start)
    return sample, start


def pack_queries(groups, heads, who, q_ref, *refs):
    outs, sem = refs[:-1], refs[-1]
    copies = []
    for j, out in enumerate(outs):
        for h in range(heads):
            start = pl.multiple_of(((who[0] ^ j) * heads + h) * HEAD_DIM, HEAD_DIM)
            copy = pltpu.make_async_copy(q_ref.at[:, pl.ds(start, HEAD_DIM)], out.at[h], sem.at[j, h])
            copy.start()
            copies.append(copy)
    for copy in copies:
        copy.wait()


def pack_grads(groups, heads, who, length, o_hbm, g_hbm, *refs):
    outs, o_ref, g_ref, sem = refs[:groups], refs[-3], refs[-2], refs[-1]
    first = pltpu.make_async_copy(o_hbm, o_ref, sem.at[0])
    second = pltpu.make_async_copy(g_hbm, g_ref, sem.at[1])
    first.start()
    second.start()
    first.wait()
    second.wait()
    rows = g_ref.shape[0]
    seq = who[0]
    position = seq * rows + lax.broadcasted_iota(jnp.int32, (rows, HEAD_DIM), 0)
    keep = position < length[0]
    for j, out in enumerate(outs):
        for h in range(heads):
            columns = pl.ds(pl.multiple_of(((seq ^ j) * heads + h) * HEAD_DIM, HEAD_DIM), HEAD_DIM)
            grad = jnp.where(keep, g_ref[:, columns].astype(F32), 0.0)
            product = grad * o_ref[:, columns].astype(F32)
            delta = jnp.sum(jnp.transpose(product), axis=0, keepdims=True)
            out[h, :rows] = grad.astype(BF16)
            out[h, rows:] = jnp.broadcast_to(delta, (DELTA_ROWS, HEAD_DIM)).astype(BF16)


def fetch(pieces, relative, target, sem):
    for index, piece in enumerate(pieces):
        @pl.when(relative == index)
        def _(piece=piece):
            pltpu.make_async_copy(piece, target, sem).start()


def spans_of(rows):
    full = rows // KEY_ROWS
    tail = rows - full * KEY_ROWS
    return [(i * KEY_ROWS, KEY_ROWS, KEY_ROWS) for i in range(full)] + [(full * KEY_ROWS, -(-tail // 16) * 16, tail)]


def dot_nt(a, b):
    return lax.dot_general(a, b, (((1,), (1,)), ((), ())), preferred_element_type=F32)


def dot_nn(a, b):
    return jnp.dot(a, b, preferred_element_type=F32)


def own_tiles(owners, slots, who, counts, perm):
    first = place_of(perm, who[1], owners)
    return [sample_at(counts, first + slot * owners, owners) for slot in range(slots)]


def weights_kernel(owners, heads, blocks, slots, who, counts, perm, own_kv, partner_kv, *refs):
    q_pieces = refs[:owners]
    stats, weights, q_buf, k_buf, k_tail, scores_buf, q_sem, k_sem = refs[owners:]
    step = pl.program_id(0)
    odd = who[0] & 1
    rows = k_buf.shape[1]
    spans = spans_of(rows)
    chunks = q_buf.shape[1] // blocks
    width = chunks * HEAD_DIM
    tiles = own_tiles(owners, slots, who, counts, perm)

    @pl.when(step == 0)
    def _():
        k_tail[...] = jnp.zeros(k_tail.shape, BF16)
        for slot in range(slots):
            @pl.when(tiles[slot][0] < owners)
            def _(slot=slot):
                fetch([own_kv.at[slot], partner_kv.at[slot]], odd, k_buf.at[slot], k_sem.at[slot])
                fetch(q_pieces, tiles[slot][0] ^ who[1], q_buf.at[slot], q_sem.at[slot])

    for slot in range(slots):
        base = slot * heads * blocks

        @pl.when((step == base) & (tiles[slot][0] < owners))
        def _(slot=slot):
            pltpu.make_async_copy(own_kv.at[slot], k_buf.at[slot], k_sem.at[slot]).wait()
            pltpu.make_async_copy(q_pieces[0], q_buf.at[slot], q_sem.at[slot]).wait()
            k_tail[:spans[-1][2]] = k_buf[slot, spans[-1][0]:]

        @pl.when((step >= base) & (step < base + heads * blocks) & (tiles[slot][0] < owners))
        def _(slot=slot, base=base):
            head, block = (step - base) // blocks, (step - base) % blocks
            query = q_buf[slot, pl.ds(block * chunks, chunks), head].reshape(width, HEAD_DIM)
            peak = jnp.full((8, width), -jnp.inf, F32)
            for low, size, used in spans:
                if size == used:
                    scores = dot_nt(k_buf[slot, low:low + size], query)
                else:
                    scores = dot_nt(k_tail[...], query)
                    row = lax.broadcasted_iota(jnp.int32, scores.shape, 0)
                    scores = jnp.where(row < used, scores, -jnp.inf)
                scores_buf[low:low + size] = scores
                peak = jnp.maximum(peak, jnp.max(scores.reshape(-1, 8, width), axis=0))
            top = jnp.max(peak, axis=0, keepdims=True) * SCALE_LOG2
            mass = jnp.zeros((8, width), F32)
            for low, size, used in spans:
                part = jnp.exp2(scores_buf[low:low + size] * SCALE_LOG2 - top)
                mass = mass + jnp.sum(part.reshape(-1, 8, width), axis=0)
                weights[0, low:low + size] = part.astype(BF16)
            total = jnp.sum(mass, axis=0, keepdims=True)
            stats[slot, 0, head, pl.ds(block, 1)] = top
            stats[slot, 1, head, pl.ds(block, 1)] = total


def slopes_kernel(owners, heads, blocks, slots, who, counts, perm, weights, own_kv, partner_kv, *refs):
    g_pieces = refs[:owners]
    slopes, turned, g_buf, kv_buf, kv_tail, k_turn, g_sem, kv_sem = refs[owners:]
    step = pl.program_id(0)
    odd = who[0] & 1
    rows = kv_buf.shape[2]
    spans = spans_of(rows)
    chunks = g_buf.shape[1] // blocks
    width = chunks * HEAD_DIM
    tiles = own_tiles(owners, slots, who, counts, perm)

    @pl.when(step == 0)
    def _():
        kv_tail[...] = jnp.zeros(kv_tail.shape, BF16)
        for slot in range(slots):
            @pl.when(tiles[slot][0] < owners)
            def _(slot=slot):
                pltpu.make_async_copy(own_kv.at[slot], kv_buf.at[slot, odd], kv_sem.at[slot, 0]).start()
                pltpu.make_async_copy(partner_kv.at[slot], kv_buf.at[slot, 1 - odd], kv_sem.at[slot, 1]).start()
                fetch(g_pieces, tiles[slot][0] ^ who[1], g_buf.at[slot], g_sem.at[slot])

    for slot in range(slots):
        base = slot * heads * blocks

        @pl.when((step == base) & (tiles[slot][0] < owners))
        def _(slot=slot):
            pltpu.make_async_copy(own_kv.at[slot], kv_buf.at[slot, odd], kv_sem.at[slot, 0]).wait()
            pltpu.make_async_copy(partner_kv.at[slot], kv_buf.at[slot, 1 - odd], kv_sem.at[slot, 1]).wait()
            pltpu.make_async_copy(g_pieces[0], g_buf.at[slot], g_sem.at[slot]).wait()
            for which in range(2):
                kv_tail[which, :spans[-1][2]] = kv_buf[slot, which, spans[-1][0]:]
            for low, size, used in spans:
                keys = kv_buf[slot, 0, low:low + size] if size == used else kv_tail[0]
                k_turn[:, low:low + size] = jnp.transpose(keys.astype(F32)).astype(BF16)

        @pl.when((step >= base) & (step < base + heads * blocks) & (tiles[slot][0] < owners))
        def _(slot=slot, base=base):
            head, block = (step - base) // blocks, (step - base) % blocks
            pieces = pl.ds(block * chunks, chunks)
            grad = g_buf[slot, pieces, head, :HEAD_DIM].reshape(width, HEAD_DIM)
            delta = jnp.concatenate(
                [g_buf[slot, block * chunks + piece, head, HEAD_DIM:].astype(F32)[:1] for piece in range(chunks)], axis=1
            )
            total = jnp.zeros((HEAD_DIM, width), F32)
            for low, size, used in spans:
                values = kv_buf[slot, 1, low:low + size] if size == used else kv_tail[1]
                slope = dot_nt(values, grad)
                bent = (weights[0, low:low + size].astype(F32) * (slope - delta)).astype(BF16)
                slopes[0, low:low + size] = bent
                total = total + dot_nn(k_turn[:, low:low + size], bent)
            turned[slot, head, :, pl.ds(pl.multiple_of(block * width, width), width)] = total.astype(BF16)


def load_stats(stats, stats_buf):
    for index, ref in enumerate(stats):
        stats_buf[2 * index:2 * index + 2] = ref[...]


def peak_and_mass(stats_buf, owners, me, perm, start, tiles, head, block):
    found = []
    for index in range(MAX_TILES):
        live = index < tiles
        place = jnp.where(live, start + index, start)
        other = perm[place & (owners - 1)] ^ me
        slot = lax.div(place, owners)
        top = stats_buf[other, slot, 0, head, pl.ds(block, 1)]
        mass = stats_buf[other, slot, 1, head, pl.ds(block, 1)]
        found.append((jnp.where(live, top, -jnp.inf), jnp.where(live, mass, 0.0)))
    top = functools.reduce(jnp.maximum, [peak for peak, _ in found])
    return top, sum(mass * jnp.exp2(peak - top) for peak, mass in found)


def sums_kernel(owners, heads, blocks, slots, slot, who, counts, perm, weights, slopes, *refs):
    stats = refs[:owners // 2]
    q_pieces, g_pieces = refs[owners // 2:owners // 2 + owners], refs[owners // 2 + owners:owners // 2 + 2 * owners]
    keep_out, send_out, stats_buf, q_buf, g_buf, sums, q_sem, g_sem = refs[owners // 2 + 2 * owners:]
    step = pl.program_id(0)
    odd, me = who[0] & 1, who[1]
    spans = spans_of(sums.shape[1])
    chunks = q_buf.shape[0] // blocks
    width = chunks * HEAD_DIM
    sample, start = own_tiles(owners, slots, who, counts, perm)[slot]
    used = sample < owners

    @pl.when((step == 0) & used)
    def _():
        fetch(q_pieces, sample ^ me, q_buf, q_sem)
        fetch(g_pieces, sample ^ me, g_buf, g_sem)
        load_stats(stats, stats_buf)
        pltpu.make_async_copy(q_pieces[0], q_buf, q_sem).wait()
        pltpu.make_async_copy(g_pieces[0], g_buf, g_sem).wait()

    @pl.when(jnp.logical_not(used))
    def _():
        keep_out[...] = jnp.zeros(keep_out.shape, BF16)
        send_out[...] = jnp.zeros(send_out.shape, BF16)

    @pl.when(used)
    def _():
        head, block = step // blocks, step % blocks
        top, mass = peak_and_mass(stats_buf, owners, me, perm, start, counts[jnp.minimum(sample, owners - 1)], head, block)
        factor = jnp.exp2(stats_buf[0, slot, 0, head, pl.ds(block, 1)] - top) / mass
        factor = jnp.transpose(jnp.broadcast_to(factor, (HEAD_DIM, width)))
        pieces = pl.ds(block * chunks, chunks)
        query = q_buf[pieces, head].reshape(width, HEAD_DIM)
        grad = g_buf[pieces, head, :HEAD_DIM].reshape(width, HEAD_DIM)
        query = (query.astype(F32) * factor * SCALE).astype(BF16)
        grad = (grad.astype(F32) * factor).astype(BF16)

        def add(which, source, right, fresh):
            for low in range(0, sums.shape[1], 2 * KEY_ROWS):
                span = slice(low, min(low + 2 * KEY_ROWS, sums.shape[1]))
                part = dot_nn(source[0, span], right)
                sums[which, span] = part if fresh else sums[which, span] + part

        for fresh in (True, False):
            @pl.when((step == 0) == fresh)
            def _(fresh=fresh):
                add(0, slopes, query, fresh)
                add(1, weights, grad, fresh)

        @pl.when(step == heads * blocks - 1)
        def _():
            keep_out[...] = sums[odd].astype(BF16)
            send_out[...] = sums[1 - odd].astype(BF16)


def route_kernel(owners, heads, blocks, slots, who, counts, perm, own, other, *refs):
    stats = refs[:owners // 2]
    outs, stats_buf = refs[owners // 2:-1], refs[-1]
    load_stats(stats, stats_buf)
    me = who[1]
    width = own.shape[3] // blocks
    found = []
    for near in range(2):
        first = place_of(perm, me ^ near, owners)
        for slot in range(slots):
            sample, start = sample_at(counts, first + slot * owners, owners)
            found.append((near, slot, sample, start, counts[jnp.minimum(sample, owners - 1)]))

    def one(step, carry):
        head, block = step // blocks, step % blocks
        columns = pl.ds(pl.multiple_of(block * width, width), width)
        scaled = []
        for near, slot, sample, start, tiles in found:
            top, mass = peak_and_mass(stats_buf, owners, me, perm, start, tiles, head, block)
            factor = jnp.exp2(stats_buf[near, slot, 0, head, pl.ds(block, 1)] - top) / mass * SCALE
            scaled.append((own, other)[near][slot, head, :, columns].astype(F32) * factor)
        for distance, out in enumerate(outs):
            target = me ^ (2 * distance)
            total = sum(jnp.where(item[2] == target, part, 0.0) for item, part in zip(found, scaled))
            out[head, :, columns] = total.astype(BF16)
        return carry

    lax.fori_loop(0, heads * blocks, one, 0)


def gather_kernel(parts, *refs):
    outs = refs[parts:]
    rows = outs[0].shape[0]
    for piece, out in enumerate(outs):
        span = slice(piece * rows, (piece + 1) * rows)
        for head in range(refs[0].shape[0]):
            total = sum(ref[head, :, span].astype(F32) for ref in refs[:parts])
            out[:, head * HEAD_DIM:(head + 1) * HEAD_DIM] = jnp.transpose(total).astype(BF16)


def place_kernel(who, *refs):
    out = refs[-1]
    for distance, ref in enumerate(refs[:-1]):
        width = ref.shape[1]
        start = pl.multiple_of((who[0] ^ distance) * width, width)
        out[:, pl.ds(start, width)] = ref[...]


def merge_kernel(slots, *refs):
    keep, got, out = refs[:slots], refs[slots:-1], refs[-1]
    for low, size, used in spans_of(out.shape[0]):
        row = lax.broadcasted_iota(jnp.int32, (slots * size, slots * size), 0)
        column = lax.broadcasted_iota(jnp.int32, (slots * size, slots * size), 1)
        source = lax.rem(row, slots) * size + lax.div(row, slots)
        order = (source == column).astype(BF16)
        total = [
            (keep[slot][low:low + size].astype(F32) + got[slot][low:low + size].astype(F32)).astype(BF16)
            for slot in range(slots)
        ]
        mixed = dot_nn(order, jnp.concatenate(total, axis=0)).astype(BF16).reshape(size, slots, HEAD_DIM)
        out[low:low + used] = mixed[:used]


def gather_pieces(block):
    count = lax.axis_size("dp")
    near = [block] + [exchange(block, "dp", distance) for distance in range(2, count, 2)]
    result = []
    for piece in near:
        result += [piece, exchange(piece, "dp", 1)]
    return result


def shards(queries, saved_output, grad_out, tile_kv, tile_count, owner_perm, text_len):
    rows_dev, features = queries.shape[1], queries.shape[2]
    groups, owners = lax.axis_size("seq"), lax.axis_size("dp")
    heads = features // HEAD_DIM // groups
    width = heads * HEAD_DIM
    text_rows = groups * rows_dev
    chunks = min(TEXT_CHUNKS, groups)
    blocks = groups // chunks
    block_rows = chunks * rows_dev
    steps = heads * blocks
    slots, tile_rows = tile_kv.shape[0], tile_kv.shape[1]
    low, tail_rows, _ = spans_of(tile_rows)[-1]
    padded = low + tail_rows
    who = jnp.stack([lax.axis_index("seq"), lax.axis_index("dp")]).astype(jnp.int32)
    work = 2 * width * text_rows * tile_rows

    q_packed = call(
        functools.partial(pack_queries, groups, heads),
        [jax.ShapeDtypeStruct((heads, rows_dev, HEAD_DIM), BF16)] * groups,
        [SMEM, ANY],
        [pltpu.SemaphoreType.DMA((groups, heads))],
        (who, queries[0]),
    )
    g_packed = call(
        functools.partial(pack_grads, groups, heads),
        [jax.ShapeDtypeStruct((heads, rows_dev + DELTA_ROWS, HEAD_DIM), BF16)] * groups,
        [SMEM, SMEM, ANY, ANY],
        [pltpu.VMEM((rows_dev, features), BF16)] * 2 + [pltpu.SemaphoreType.DMA((2,))],
        (who, text_len, saved_output[0], grad_out[0]),
    )

    def over_seq(pieces):
        return jnp.stack([pieces[0]] + [exchange(pieces[j], "seq", j) for j in range(1, groups)])

    q_all = gather_pieces(over_seq(q_packed))
    partner_kv = exchange(tile_kv, "seq", 1)
    g_all = gather_pieces(over_seq(g_packed))

    known = (who, tile_count, owner_perm)
    q_scratch = pltpu.VMEM((slots,) + q_all[0].shape, BF16)
    g_scratch = pltpu.VMEM((slots,) + g_all[0].shape, BF16)
    stack_shape = jax.ShapeDtypeStruct((slots * steps, padded, block_rows), BF16)
    stack_spec = pl.BlockSpec((1, padded, block_rows), lambda i: (i, 0, 0))
    stats_shape = (slots, 2, heads, blocks, block_rows)

    stats, weights = call(
        functools.partial(weights_kernel, owners, heads, blocks, slots),
        [jax.ShapeDtypeStruct(stats_shape, F32), stack_shape],
        [SMEM] * 3 + [ANY] * (2 + owners),
        [
            q_scratch,
            pltpu.VMEM((slots, tile_rows, HEAD_DIM), BF16),
            pltpu.VMEM((tail_rows, HEAD_DIM), BF16),
            pltpu.VMEM((padded, block_rows), F32),
            pltpu.SemaphoreType.DMA((slots,)),
            pltpu.SemaphoreType.DMA((slots,)),
        ],
        (*known, tile_kv, partner_kv, *q_all),
        out_specs=[VMEM, stack_spec],
        grid=(slots * steps,),
        megabytes=32,
        flops=slots * work,
    )
    pair = jnp.stack([stats, exchange(stats, "dp", 1)])
    all_stats = [pair] + [exchange(pair, "dp", d) for d in range(2, owners, 2)]

    slopes, turned = call(
        functools.partial(slopes_kernel, owners, heads, blocks, slots),
        [stack_shape, jax.ShapeDtypeStruct((slots, heads, HEAD_DIM, text_rows), BF16)],
        [SMEM] * 3 + [stack_spec] + [ANY] * (2 + owners),
        [
            g_scratch,
            pltpu.VMEM((slots, 2, tile_rows, HEAD_DIM), BF16),
            pltpu.VMEM((2, tail_rows, HEAD_DIM), BF16),
            pltpu.VMEM((HEAD_DIM, -(-padded // HEAD_DIM) * HEAD_DIM), BF16),
            pltpu.SemaphoreType.DMA((slots,)),
            pltpu.SemaphoreType.DMA((slots, 2)),
        ],
        (*known, weights, tile_kv, partner_kv, *g_all),
        out_specs=[stack_spec, VMEM],
        grid=(slots * steps,),
        megabytes=32,
        flops=2 * slots * work,
    )

    stats_scratch = pltpu.VMEM((owners,) + stats_shape, F32)
    routed = call(
        functools.partial(route_kernel, owners, heads, blocks, slots),
        [jax.ShapeDtypeStruct((heads, HEAD_DIM, text_rows), BF16)] * (owners // 2),
        [SMEM] * 3 + [VMEM] * (2 + owners // 2),
        [stats_scratch],
        (*known, turned, exchange(turned, "dp", 1), *all_stats),
        megabytes=32,
    )

    kept, got = [], []
    for slot in range(slots):
        part_spec = pl.BlockSpec((1, padded, block_rows), lambda i, slot=slot: (slot * steps + i, 0, 0))
        keep, send = call(
            functools.partial(sums_kernel, owners, heads, blocks, slots, slot),
            [jax.ShapeDtypeStruct((padded, HEAD_DIM), BF16)] * 2,
            [SMEM] * 3 + [part_spec] * 2 + [VMEM] * (owners // 2) + [ANY] * (2 * owners),
            [
                stats_scratch,
                pltpu.VMEM(q_all[0].shape, BF16),
                pltpu.VMEM(g_all[0].shape, BF16),
                pltpu.VMEM((2, padded, HEAD_DIM), F32),
                pltpu.SemaphoreType.DMA(()),
                pltpu.SemaphoreType.DMA(()),
            ],
            (*known, weights, slopes, *all_stats, *q_all, *g_all),
            out_specs=[VMEM, VMEM],
            grid=(steps,),
            megabytes=32,
            flops=2 * work,
        )
        kept.append(keep)
        got.append(exchange(send, "seq", 1))

    sums = [routed[0]] + [exchange(routed[d], "dp", 2 * d) for d in range(1, owners // 2)]
    cut = call(
        functools.partial(gather_kernel, len(sums)),
        [jax.ShapeDtypeStruct((rows_dev, width), BF16)] * groups,
        [VMEM] * len(sums),
        [],
        sums,
        megabytes=32,
    )
    back = [cut[0]] + [exchange(cut[j], "seq", j) for j in range(1, groups)]
    grad_queries = call(
        place_kernel,
        jax.ShapeDtypeStruct((rows_dev, features), BF16),
        [SMEM] + [VMEM] * groups,
        [],
        (who, *back),
    )
    grad_tiles = call(
        functools.partial(merge_kernel, slots),
        jax.ShapeDtypeStruct((tile_rows, slots, HEAD_DIM), BF16),
        [VMEM] * (2 * slots),
        [],
        (*kept, *got),
    )
    return (grad_queries[None], jnp.transpose(grad_tiles, (1, 0, 2)))


def solution(mesh):
    placed = (
        P("dp", "seq", None),
        P("dp", "seq", None),
        P("dp", "seq", None),
        P("dp", None, "seq"),
        P(),
        P(),
        P("dp"),
    )
    return jax.shard_map(
        shards,
        mesh=mesh,
        in_specs=placed,
        out_specs=(P("dp", "seq", None), P("dp", None, "seq")),
        check_vma=False,
    )
```

```python
import functools
import math

import jax
import jax.numpy as jnp
from jax import lax
from jax.experimental import pallas as pl
from jax.experimental.pallas import tpu as pltpu
from jax.sharding import PartitionSpec as P

HEAD_DIM = 128
MAX_TILES = 4
KEY_ROWS = 256
TEXT_CHUNKS = 4
DELTA_ROWS = 16
SCALE = 1.0 / math.sqrt(HEAD_DIM)
SCALE_LOG2 = SCALE / math.log(2.0)
BF16 = jnp.bfloat16
F32 = jnp.float32

SMEM = pl.BlockSpec(memory_space=pltpu.SMEM)
VMEM = pl.BlockSpec(memory_space=pltpu.VMEM)
ANY = pl.BlockSpec(memory_space=pl.ANY)
HBM = pl.BlockSpec(memory_space=pltpu.HBM)


def exchange(block, axis, distance):
    count = lax.axis_size(axis)
    return lax.ppermute(block, axis, [(i, i ^ distance) for i in range(count)])


def call(kernel, out_shape, in_specs, scratch, args, out_specs=None, grid=(), megabytes=16, flops=0, moved=0):
    many = isinstance(out_shape, (list, tuple))
    if out_specs is None:
        out_specs = [VMEM] * len(out_shape) if many else VMEM
    return pl.pallas_call(
        kernel,
        out_shape=out_shape,
        in_specs=in_specs,
        out_specs=out_specs,
        grid=grid,
        scratch_shapes=scratch,
        compiler_params=pltpu.CompilerParams(vmem_limit_bytes=megabytes << 20),
        cost_estimate=pl.CostEstimate(flops=flops, bytes_accessed=moved, transcendentals=0),
    )(*args)


def place_of(perm_ref, owner, owners):
    first = jnp.int32(0)
    for index in range(owners):
        first = first + jnp.where(perm_ref[index] == owner, index, 0)
    return first


def sample_at(count_ref, place, samples):
    end, sample, start = jnp.int32(0), jnp.int32(0), jnp.int32(0)
    for index in range(samples):
        end = end + count_ref[index]
        passed = place >= end
        sample = sample + passed.astype(jnp.int32)
        start = jnp.where(passed, end, start)
    return sample, start


def pack_kernel(heads, who, length, *refs):
    inputs, outs, buffers, sem = refs[:3], refs[3:-4], refs[-4:-1], refs[-1]
    copies = [pltpu.make_async_copy(a, b, sem.at[i]) for i, (a, b) in enumerate(zip(inputs, buffers))]
    for copy in copies:
        copy.start()
    for copy in copies:
        copy.wait()
    q_ref, o_ref, g_ref = buffers
    rows = q_ref.shape[0]
    seq = who[0]
    position = seq * rows + lax.broadcasted_iota(jnp.int32, (rows, HEAD_DIM), 0)
    keep = position < length[0]
    for j, out in enumerate(outs):
        for h in range(heads):
            columns = pl.ds(pl.multiple_of(((seq ^ j) * heads + h) * HEAD_DIM, HEAD_DIM), HEAD_DIM)
            grad = jnp.where(keep, g_ref[:, columns].astype(F32), 0.0)
            product = grad * o_ref[:, columns].astype(F32)
            delta = jnp.sum(jnp.transpose(product), axis=0, keepdims=True)
            out[h, :rows] = q_ref[:, columns]
            out[h, rows:2 * rows] = grad.astype(BF16)
            out[h, 2 * rows:] = jnp.broadcast_to(delta, (DELTA_ROWS, HEAD_DIM)).astype(BF16)


def stack_kernel(count, *refs):
    out, sem = refs[-2], refs[-1]
    copies = [pltpu.make_async_copy(refs[i], out.at[i], sem.at[i]) for i in range(count)]
    for copy in copies:
        copy.start()
    for copy in copies:
        copy.wait()


def fetch(pieces, relative, target, sem):
    for index, piece in enumerate(pieces):
        @pl.when(relative == index)
        def _(piece=piece):
            pltpu.make_async_copy(piece, target, sem).start()


def spans_of(rows):
    full = rows // KEY_ROWS
    tail = rows - full * KEY_ROWS
    return [(i * KEY_ROWS, KEY_ROWS, KEY_ROWS) for i in range(full)] + [(full * KEY_ROWS, -(-tail // 16) * 16, tail)]


def dot_nt(a, b):
    return lax.dot_general(a, b, (((1,), (1,)), ((), ())), preferred_element_type=F32)


def dot_nn(a, b):
    return jnp.dot(a, b, preferred_element_type=F32)


def own_tiles(owners, slots, who, counts, perm):
    first = place_of(perm, who[1], owners)
    return [sample_at(counts, first + slot * owners, owners) for slot in range(slots)]


def tiles_kernel(slots, who, own, partner, keys, values, turned):
    for odd in range(2):
        @pl.when((who[0] & 1) == odd)
        def _(odd=odd):
            for slot in range(slots):
                for source, target in (((own, partner)[odd], keys), ((own, partner)[1 - odd], values)):
                    for low, size, used in spans_of(own.shape[1]):
                        if size != used:
                            target[slot, low:] = jnp.zeros((size, HEAD_DIM), BF16)
                        target[slot, low:low + used] = source[slot, low:low + used]
    for slot in range(slots):
        for low, size, _ in spans_of(own.shape[1]):
            turned[slot, :, low:low + size] = jnp.transpose(keys[slot, low:low + size].astype(F32)).astype(BF16)


def weights_kernel(owners, heads, blocks, slots, rows, who, counts, perm, keys, *refs):
    pieces = refs[:owners]
    stats, weights, text_buf, scores_buf, sem = refs[owners:]
    step = pl.program_id(0)
    spans = spans_of(rows)
    chunks = text_buf.shape[1] // blocks
    width = chunks * HEAD_DIM
    tiles = own_tiles(owners, slots, who, counts, perm)

    @pl.when(step == 0)
    def _():
        for slot in range(slots):
            @pl.when(tiles[slot][0] < owners)
            def _(slot=slot):
                fetch(pieces, tiles[slot][0] ^ who[1], text_buf.at[slot], sem.at[slot])

    for slot in range(slots):
        base = slot * heads * blocks

        @pl.when((step == base) & (tiles[slot][0] < owners))
        def _(slot=slot):
            pltpu.make_async_copy(pieces[0], text_buf.at[slot], sem.at[slot]).wait()

        @pl.when((step >= base) & (step < base + heads * blocks) & (tiles[slot][0] < owners))
        def _(slot=slot, base=base):
            head, block = (step - base) // blocks, (step - base) % blocks
            query = text_buf[slot, pl.ds(block * chunks, chunks), head, :HEAD_DIM].reshape(width, HEAD_DIM)
            peak = jnp.full((8, width), -jnp.inf, F32)
            for low, size, used in spans:
                scores = dot_nt(keys[slot, low:low + size], query)
                if size != used:
                    row = lax.broadcasted_iota(jnp.int32, scores.shape, 0)
                    scores = jnp.where(row < used, scores, -jnp.inf)
                scores_buf[low:low + size] = scores
                peak = jnp.maximum(peak, jnp.max(scores.reshape(-1, 8, width), axis=0))
            top = jnp.max(peak, axis=0, keepdims=True) * SCALE_LOG2
            mass = jnp.zeros((8, width), F32)
            for low, size, used in spans:
                part = jnp.exp2(scores_buf[low:low + size] * SCALE_LOG2 - top)
                mass = mass + jnp.sum(part.reshape(-1, 8, width), axis=0)
                weights[0, low:low + size] = part.astype(BF16)
            stats[slot, 0, head, pl.ds(block, 1)] = top
            stats[slot, 1, head, pl.ds(block, 1)] = jnp.sum(mass, axis=0, keepdims=True)


def slopes_kernel(owners, heads, blocks, slots, slot, rows, who, counts, perm, weights, values, keys_turned, *refs):
    pieces = refs[:owners]
    slopes, turned, text_buf, sem = refs[-4:]
    step = pl.program_id(0)
    spans = spans_of(rows)
    chunks = text_buf.shape[0] // blocks
    width = chunks * HEAD_DIM
    sample = own_tiles(owners, slots, who, counts, perm)[slot][0]

    @pl.when((step == 0) & (sample < owners))
    def _():
        fetch(pieces, sample ^ who[1], text_buf, sem)
        pltpu.make_async_copy(pieces[0], text_buf, sem).wait()

    @pl.when(sample < owners)
    def _():
        head, block = step // blocks, step % blocks
        grad = text_buf[pl.ds(block * chunks, chunks), head, HEAD_DIM:2 * HEAD_DIM].reshape(width, HEAD_DIM)
        delta = jnp.concatenate(
            [text_buf[block * chunks + piece, head, 2 * HEAD_DIM:].astype(F32)[:1] for piece in range(chunks)], axis=1
        )
        for low, size, used in spans:
            slope = dot_nt(values[slot, low:low + size], grad)
            slopes[0, low:low + size] = (weights[0, low:low + size].astype(F32) * (slope - delta)).astype(BF16)
        total = dot_nn(keys_turned[slot, :, :slopes.shape[1]], slopes[0])
        turned[head, :, pl.ds(pl.multiple_of(block * width, width), width)] = total.astype(BF16)


def load_stats(stats, stats_buf):
    for index, ref in enumerate(stats):
        stats_buf[2 * index:2 * index + 2] = ref[...]


def peak_and_mass(stats_buf, owners, me, perm, start, tiles, head, block):
    found = []
    for index in range(MAX_TILES):
        live = index < tiles
        place = jnp.where(live, start + index, start)
        other = perm[place & (owners - 1)] ^ me
        slot = lax.div(place, owners)
        top = stats_buf[other, slot, 0, head, pl.ds(block, 1)]
        mass = stats_buf[other, slot, 1, head, pl.ds(block, 1)]
        found.append((jnp.where(live, top, -jnp.inf), jnp.where(live, mass, 0.0)))
    top = functools.reduce(jnp.maximum, [peak for peak, _ in found])
    return top, sum(mass * jnp.exp2(peak - top) for peak, mass in found)


def sums_kernel(owners, heads, blocks, slots, slot, who, counts, perm, *refs):
    weights, slopes, refs = refs[:2], refs[2:4], refs[4:]
    chips = owners // 2
    stats, refs = (refs[:chips], refs[chips:2 * chips]), refs[2 * chips:]
    pieces, refs = (refs[:owners], refs[owners:2 * owners]), refs[2 * owners:]
    keep_out, send_out, stats_buf, text_buf, sums, sem = refs
    step = pl.program_id(0)
    odd, me = who[0] & 1, who[1]
    steps = heads * blocks
    chunks = text_buf.shape[1] // blocks
    width = chunks * HEAD_DIM
    sample, start = own_tiles(owners, slots, who, counts, perm)[slot]
    used = sample < owners

    @pl.when((step == 0) & used)
    def _():
        for half in range(2):
            fetch(pieces[half], sample ^ me, text_buf.at[half], sem.at[half])
            load_stats(stats[half], stats_buf.at[half])
        for half in range(2):
            pltpu.make_async_copy(pieces[half][0], text_buf.at[half], sem.at[half]).wait()

    @pl.when(jnp.logical_not(used))
    def _():
        keep_out[...] = jnp.zeros(keep_out.shape, BF16)
        send_out[...] = jnp.zeros(send_out.shape, BF16)

    for half in range(2):
        @pl.when(used & (step >= half * steps) & (step < (half + 1) * steps))
        def _(half=half):
            inner = step - half * steps
            head, block = inner // blocks, inner % blocks
            tiles = counts[jnp.minimum(sample, owners - 1)]
            top, mass = peak_and_mass(stats_buf.at[half], owners, me, perm, start, tiles, head, block)
            factor = jnp.exp2(stats_buf[half, 0, slot, 0, head, pl.ds(block, 1)] - top) / mass
            factor = jnp.transpose(jnp.broadcast_to(factor, (HEAD_DIM, width)))
            where = pl.ds(block * chunks, chunks)
            query = text_buf[half, where, head, :HEAD_DIM].reshape(width, HEAD_DIM)
            grad = text_buf[half, where, head, HEAD_DIM:2 * HEAD_DIM].reshape(width, HEAD_DIM)
            query = (query.astype(F32) * factor * SCALE).astype(BF16)
            grad = (grad.astype(F32) * factor).astype(BF16)

            def add(which, source, right, fresh):
                for low in range(0, sums.shape[1], 2 * KEY_ROWS):
                    span = slice(low, min(low + 2 * KEY_ROWS, sums.shape[1]))
                    part = dot_nn(source[0, span], right)
                    sums[which, span] = part if fresh else sums[which, span] + part

            for fresh in (True, False):
                if half and fresh:
                    continue

                @pl.when((step == 0) == fresh)
                def _(fresh=fresh):
                    add(0, slopes[half], query, fresh)
                    add(1, weights[half], grad, fresh)

    @pl.when(used & (step == 2 * steps - 1))
    def _():
        keep_out[...] = sums[odd].astype(BF16)
        send_out[...] = sums[1 - odd].astype(BF16)


def route_kernel(owners, heads, blocks, slots, who, counts, perm, *refs):
    parts, refs = (refs[:slots], refs[slots:2 * slots]), refs[2 * slots:]
    stats = refs[:owners // 2]
    outs, stats_buf = refs[owners // 2:-1], refs[-1]
    load_stats(stats, stats_buf)
    me = who[1]
    width = parts[0][0].shape[2] // blocks
    found = []
    for near in range(2):
        first = place_of(perm, me ^ near, owners)
        for slot in range(slots):
            sample, start = sample_at(counts, first + slot * owners, owners)
            found.append((near, slot, sample, start, counts[jnp.minimum(sample, owners - 1)]))

    def one(step, carry):
        head, block = step // blocks, step % blocks
        columns = pl.ds(pl.multiple_of(block * width, width), width)
        scaled = []
        for near, slot, sample, start, tiles in found:
            top, mass = peak_and_mass(stats_buf, owners, me, perm, start, tiles, head, block)
            factor = jnp.exp2(stats_buf[near, slot, 0, head, pl.ds(block, 1)] - top) / mass * SCALE
            scaled.append(parts[near][slot][head, :, columns].astype(F32) * factor)
        for distance, out in enumerate(outs):
            target = me ^ (2 * distance)
            total = sum(jnp.where(item[2] == target, part, 0.0) for item, part in zip(found, scaled))
            out[head, :, columns] = total.astype(BF16)
        return carry

    lax.fori_loop(0, heads * blocks, one, 0)


def gather_kernel(parts, *refs):
    outs = refs[parts:]
    rows = outs[0].shape[0]
    for piece, out in enumerate(outs):
        span = slice(piece * rows, (piece + 1) * rows)
        for head in range(refs[0].shape[0]):
            total = sum(ref[head, :, span].astype(F32) for ref in refs[:parts])
            out[:, head * HEAD_DIM:(head + 1) * HEAD_DIM] = jnp.transpose(total).astype(BF16)


def place_kernel(who, *refs):
    out = refs[-1]
    for distance, ref in enumerate(refs[:-1]):
        width = ref.shape[1]
        start = pl.multiple_of((who[0] ^ distance) * width, width)
        out[:, pl.ds(start, width)] = ref[...]


def merge_kernel(slots, *refs):
    keep, got, out = refs[:slots], refs[slots:-1], refs[-1]
    for low, size, used in spans_of(out.shape[0]):
        row = lax.broadcasted_iota(jnp.int32, (slots * size, slots * size), 0)
        column = lax.broadcasted_iota(jnp.int32, (slots * size, slots * size), 1)
        source = lax.rem(row, slots) * size + lax.div(row, slots)
        order = (source == column).astype(BF16)
        total = [
            (keep[slot][low:low + size].astype(F32) + got[slot][low:low + size].astype(F32)).astype(BF16)
            for slot in range(slots)
        ]
        mixed = dot_nn(order, jnp.concatenate(total, axis=0)).astype(BF16).reshape(size, slots, HEAD_DIM)
        out[low:low + used] = mixed[:used]


def shards(queries, saved_output, grad_out, tile_kv, tile_count, owner_perm, text_len):
    rows_dev, features = queries.shape[1], queries.shape[2]
    groups, owners = lax.axis_size("seq"), lax.axis_size("dp")
    heads = features // HEAD_DIM // groups
    width = heads * HEAD_DIM
    each = groups // 2
    chunks = min(TEXT_CHUNKS, each)
    blocks = each // chunks
    half_rows, block_rows = each * rows_dev, chunks * rows_dev
    steps = heads * blocks
    slots, tile_rows = tile_kv.shape[0], tile_kv.shape[1]
    low, tail_rows, _ = spans_of(tile_rows)[-1]
    padded = low + tail_rows
    who = jnp.stack([lax.axis_index("seq"), lax.axis_index("dp")]).astype(jnp.int32)
    known = (who, tile_count, owner_perm)
    cost = 10**9

    piece_shape = (heads, 2 * rows_dev + DELTA_ROWS, HEAD_DIM)
    packed = call(
        functools.partial(pack_kernel, heads),
        [jax.ShapeDtypeStruct(piece_shape, BF16)] * groups,
        [SMEM, SMEM] + [HBM] * 3,
        [pltpu.VMEM((rows_dev, features), BF16)] * 3 + [pltpu.SemaphoreType.DMA((3,))],
        (who, text_len, queries[0], saved_output[0], grad_out[0]),
        flops=2 * cost,
    )
    pieces = [packed[0]] + [exchange(packed[j], "seq", j) for j in range(1, groups)]
    partner_kv = exchange(tile_kv, "seq", 1)

    text, first = [], ()
    for half in range(2):
        mine = call(
            functools.partial(stack_kernel, each),
            jax.ShapeDtypeStruct((each,) + piece_shape, BF16),
            [ANY] * (each + len(first)),
            [pltpu.SemaphoreType.DMA((each,))],
            (*pieces[half * each:(half + 1) * each], *first),
        )
        near = [mine] + [exchange(mine, "dp", d) for d in range(2, owners, 2)]
        all_near = []
        for piece in near:
            all_near += [piece, exchange(piece, "dp", 1)]
        first = (all_near[1],)
        text.append(all_near)

    tile_shape = jax.ShapeDtypeStruct((slots, padded, HEAD_DIM), BF16)
    turn_shape = jax.ShapeDtypeStruct((slots, HEAD_DIM, -(-padded // HEAD_DIM) * HEAD_DIM), BF16)
    keys, values, keys_turned = call(
        functools.partial(tiles_kernel, slots),
        [tile_shape, tile_shape, turn_shape],
        [SMEM] + [VMEM] * 2,
        [],
        (who, tile_kv, partner_kv),
        flops=cost,
    )

    stats_shape = (slots, 2, heads, blocks, block_rows)
    text_shape = (each,) + piece_shape
    all_stats, weights = [], []
    slopes, routed = [[None, None] for _ in range(slots)], []

    def stack_spec(first_block, count):
        return pl.BlockSpec((1, padded, block_rows), lambda i: (first_block + jnp.clip(i, 0, count - 1), 0, 0))

    for half in range(2):
        stats, weight = call(
            functools.partial(weights_kernel, owners, heads, blocks, slots, tile_rows),
            [
                jax.ShapeDtypeStruct(stats_shape, F32),
                jax.ShapeDtypeStruct((slots * steps, padded, block_rows), BF16),
            ],
            [SMEM] * 3 + [VMEM] + [ANY] * owners,
            [
                pltpu.VMEM((slots,) + text_shape, BF16),
                pltpu.VMEM((padded, block_rows), F32),
                pltpu.SemaphoreType.DMA((slots,)),
            ],
            (*known, keys, *text[half]),
            out_specs=[VMEM, stack_spec(0, slots * steps)],
            grid=(slots * steps,),
            megabytes=32,
            flops=3 * cost,
        )
        weights.append(weight)
        pair = jnp.stack([stats, exchange(stats, "dp", 1)])
        shared = [pair] + [exchange(pair, "dp", d) for d in range(2, owners, 2)]
        all_stats.append(shared)

        parts, others = [], []
        for slot in range(slots):
            order = shared[1:] if slot else shared[:1]
            slope, part = call(
                functools.partial(slopes_kernel, owners, heads, blocks, slots, slot, tile_rows),
                [
                    jax.ShapeDtypeStruct((steps, padded, block_rows), BF16),
                    jax.ShapeDtypeStruct((heads, HEAD_DIM, half_rows), BF16),
                ],
                [SMEM] * 3 + [stack_spec(slot * steps, steps)] + [VMEM] * 2 + [ANY] * (owners + len(order)),
                [pltpu.VMEM(text_shape, BF16), pltpu.SemaphoreType.DMA(())],
                (*known, weight, values, keys_turned, *text[half], *order),
                out_specs=[stack_spec(0, steps), VMEM],
                grid=(steps,),
                megabytes=32,
                flops=2 * cost,
            )
            slopes[slot][half] = slope
            parts.append(part)
            others.append(exchange(part, "dp", 1))

        routed.append(
            call(
                functools.partial(route_kernel, owners, heads, blocks, slots),
                [jax.ShapeDtypeStruct((heads, HEAD_DIM, half_rows), BF16)] * (owners // 2),
                [SMEM] * 3 + [VMEM] * (2 * slots + owners // 2),
                [pltpu.VMEM((owners,) + stats_shape, F32)],
                (*known, *parts, *others, *shared),
                megabytes=32,
                flops=cost,
            )
        )

    kept, got = [], []
    for slot in range(slots):
        weight_specs = [
            pl.BlockSpec(
                (1, padded, block_rows),
                lambda i, half=half: (slot * steps + jnp.clip(i - half * steps, 0, steps - 1), 0, 0),
            )
            for half in range(2)
        ]
        slope_specs = [
            pl.BlockSpec(
                (1, padded, block_rows), lambda i, half=half: (jnp.clip(i - half * steps, 0, steps - 1), 0, 0)
            )
            for half in range(2)
        ]
        keep, send = call(
            functools.partial(sums_kernel, owners, heads, blocks, slots, slot),
            [jax.ShapeDtypeStruct((padded, HEAD_DIM), BF16)] * 2,
            [SMEM] * 3 + weight_specs + slope_specs + [VMEM] * owners + [ANY] * (2 * owners),
            [
                pltpu.VMEM((2, owners) + stats_shape, F32),
                pltpu.VMEM((2,) + text_shape, BF16),
                pltpu.VMEM((2, padded, HEAD_DIM), F32),
                pltpu.SemaphoreType.DMA((2,)),
            ],
            (*known, *weights, *slopes[slot], *all_stats[0], *all_stats[1], *text[0], *text[1]),
            grid=(2 * steps,),
            megabytes=32,
            flops=4 * cost,
        )
        kept.append(keep)
        got.append(exchange(send, "seq", 1))

    back = []
    for half in range(2):
        sums = [routed[half][0]] + [exchange(routed[half][d], "dp", 2 * d) for d in range(1, owners // 2)]
        cut = call(
            functools.partial(gather_kernel, len(sums)),
            [jax.ShapeDtypeStruct((rows_dev, width), BF16)] * each,
            [VMEM] * len(sums),
            [],
            sums,
            megabytes=32,
        )
        for index, piece in enumerate(cut):
            j = half * each + index
            back.append(exchange(piece, "seq", j) if j else piece)
    grad_queries = call(
        place_kernel,
        jax.ShapeDtypeStruct((rows_dev, features), BF16),
        [SMEM] + [VMEM] * groups,
        [],
        (who, *back),
    )
    grad_tiles = call(
        functools.partial(merge_kernel, slots),
        jax.ShapeDtypeStruct((tile_rows, slots, HEAD_DIM), BF16),
        [VMEM] * (2 * slots),
        [],
        (*kept, *got),
        flops=2 * cost,
    )
    return (grad_queries[None], jnp.transpose(grad_tiles, (1, 0, 2)))


def solution(mesh):
    placed = (
        P("dp", "seq", None),
        P("dp", "seq", None),
        P("dp", "seq", None),
        P("dp", None, "seq"),
        P(),
        P(),
        P("dp"),
    )
    return jax.shard_map(
        shards,
        mesh=mesh,
        in_specs=placed,
        out_specs=(P("dp", "seq", None), P("dp", None, "seq")),
        check_vma=False,
    )
```

```python
import functools
import math

import jax
import jax.numpy as jnp
from jax import lax
from jax.experimental import pallas as pl
from jax.experimental.pallas import tpu as pltpu
from jax.sharding import PartitionSpec as P

HEAD_DIM = 128
MAX_TILES = 4
KEY_ROWS = 256
TEXT_CHUNKS = 4
DELTA_ROWS = 16
NOTE_ROWS = 16
LOWEST = -1e30
SCALE = 1.0 / math.sqrt(HEAD_DIM)
SCALE_LOG2 = SCALE / math.log(2.0)
BF16 = jnp.bfloat16
F32 = jnp.float32

SMEM = pl.BlockSpec(memory_space=pltpu.SMEM)
VMEM = pl.BlockSpec(memory_space=pltpu.VMEM)
ANY = pl.BlockSpec(memory_space=pl.ANY)
HBM = pl.BlockSpec(memory_space=pltpu.HBM)


def exchange(block, axis, distance):
    count = lax.axis_size(axis)
    return lax.ppermute(block, axis, [(i, i ^ distance) for i in range(count)])


def call(kernel, out_shape, in_specs, scratch, args, out_specs=None, grid=(), megabytes=16, cost=0):
    many = isinstance(out_shape, (list, tuple))
    if out_specs is None:
        out_specs = [VMEM] * len(out_shape) if many else VMEM
    return pl.pallas_call(
        kernel,
        out_shape=out_shape,
        in_specs=in_specs,
        out_specs=out_specs,
        grid=grid,
        name=getattr(kernel, "func", kernel).__name__,
        scratch_shapes=scratch,
        compiler_params=pltpu.CompilerParams(vmem_limit_bytes=megabytes << 20),
        cost_estimate=pl.CostEstimate(flops=cost * 10**9, bytes_accessed=0, transcendentals=0),
    )(*args)


def place_of(perm_ref, owner, owners):
    first = jnp.int32(0)
    for index in range(owners):
        first = first + jnp.where(perm_ref[index] == owner, index, 0)
    return first


def sample_at(count_ref, place, samples):
    end, sample, start = jnp.int32(0), jnp.int32(0), jnp.int32(0)
    for index in range(samples):
        end = end + count_ref[index]
        passed = place >= end
        sample = sample + passed.astype(jnp.int32)
        start = jnp.where(passed, end, start)
    return sample, start


def pack_kernel(heads, who, length, *refs):
    inputs, outs, buffers, sem = refs[:3], refs[3:-4], refs[-4:-1], refs[-1]
    copies = [pltpu.make_async_copy(a, b, sem.at[i]) for i, (a, b) in enumerate(zip(inputs, buffers))]
    for copy in copies:
        copy.start()
    for copy in copies:
        copy.wait()
    q_ref, o_ref, g_ref = buffers
    rows = q_ref.shape[0]
    seq = who[0]
    position = seq * rows + lax.broadcasted_iota(jnp.int32, (rows, HEAD_DIM), 0)
    keep = position < length[0]
    for j, out in enumerate(outs):
        for h in range(heads):
            columns = pl.ds(pl.multiple_of(((seq ^ j) * heads + h) * HEAD_DIM, HEAD_DIM), HEAD_DIM)
            grad = jnp.where(keep, g_ref[:, columns].astype(F32), 0.0)
            product = grad * o_ref[:, columns].astype(F32)
            delta = jnp.sum(jnp.transpose(product), axis=0, keepdims=True)
            out[h, :rows] = q_ref[:, columns]
            out[h, rows:2 * rows] = grad.astype(BF16)
            out[h, 2 * rows:] = jnp.broadcast_to(delta, (DELTA_ROWS, HEAD_DIM)).astype(BF16)


def stack_kernel(count, rows, *refs):
    out, sem = refs[-2], refs[-1]
    copies = [pltpu.make_async_copy(refs[i].at[:, rows], out.at[i], sem.at[i]) for i in range(count)]
    for copy in copies:
        copy.start()
    for copy in copies:
        copy.wait()


def join_kernel(count, *refs):
    out, sem = refs[-2], refs[-1]
    copies = [pltpu.make_async_copy(refs[i], out.at[i], sem.at[i]) for i in range(count)]
    for copy in copies:
        copy.start()
    for copy in copies:
        copy.wait()


def fetch(pieces, relative, target, sem):
    for core, piece in enumerate(pieces):
        @pl.when((relative & 1) == core)
        def _(piece=piece):
            pltpu.make_async_copy(piece.at[lax.shift_right_logical(relative, 1)], target, sem).start()


def spans_of(rows):
    full = rows // KEY_ROWS
    tail = rows - full * KEY_ROWS
    return [(i * KEY_ROWS, KEY_ROWS, KEY_ROWS) for i in range(full)] + [(full * KEY_ROWS, -(-tail // 16) * 16, tail)]


def dot_nt(a, b):
    return lax.dot_general(a, b, (((1,), (1,)), ((), ())), preferred_element_type=F32)


def dot_nn(a, b):
    return jnp.dot(a, b, preferred_element_type=F32)


def own_tiles(owners, slots, who, counts, perm):
    first = place_of(perm, who[1], owners)
    return [sample_at(counts, first + slot * owners, owners) for slot in range(slots)]


def pad_kernel(tiles, *refs):
    out = refs[-1]
    for slot in range(tiles.shape[0]):
        for low, size, used in spans_of(tiles.shape[1]):
            if size != used:
                out[slot, low:] = jnp.zeros((size, HEAD_DIM), BF16)
            out[slot, low:low + used] = tiles[slot, low:low + used]


def tiles_kernel(slots, rows, who, own, partner, keys, values, turned):
    for odd in range(2):
        @pl.when((who[0] & 1) == odd)
        def _(odd=odd):
            keys[...] = (own, partner)[odd][...]
            values[...] = (own, partner)[1 - odd][...]
    for slot in range(slots):
        for low, size, _ in spans_of(rows):
            turned[slot, :, low:low + size] = jnp.transpose(keys[slot, low:low + size].astype(F32)).astype(BF16)


def weights_kernel(owners, heads, blocks, slots, rows, who, counts, perm, keys, *refs):
    pieces = refs[:2]
    stats, weights, text_buf, scores_buf, sem = refs[2:]
    step = pl.program_id(0)
    spans = spans_of(rows)
    chunks = text_buf.shape[1] // blocks
    width = chunks * HEAD_DIM
    tiles = own_tiles(owners, slots, who, counts, perm)

    @pl.when(step == 0)
    def _():
        for slot in range(slots):
            @pl.when(tiles[slot][0] < owners)
            def _(slot=slot):
                fetch(pieces, tiles[slot][0] ^ who[1], text_buf.at[slot], sem.at[slot])

    for slot in range(slots):
        base = slot * heads * blocks

        @pl.when((step == base) & (tiles[slot][0] < owners))
        def _(slot=slot):
            pltpu.make_async_copy(pieces[0].at[0], text_buf.at[slot], sem.at[slot]).wait()

        @pl.when((step >= base) & (step < base + heads * blocks) & (tiles[slot][0] < owners))
        def _(slot=slot, base=base):
            head, block = (step - base) // blocks, (step - base) % blocks
            query = text_buf[slot, pl.ds(block * chunks, chunks), head].reshape(width, HEAD_DIM)
            peak = jnp.full((8, width), -jnp.inf, F32)
            for low, size, used in spans:
                scores = dot_nt(keys[slot, low:low + size], query)
                if size != used:
                    row = lax.broadcasted_iota(jnp.int32, scores.shape, 0)
                    scores = jnp.where(row < used, scores, -jnp.inf)
                scores_buf[low:low + size] = scores
                peak = jnp.maximum(peak, jnp.max(scores.reshape(-1, 8, width), axis=0))
            top = jnp.max(peak, axis=0, keepdims=True) * SCALE_LOG2
            mass = jnp.zeros((8, width), F32)
            for low, size, used in spans:
                part = jnp.exp2(scores_buf[low:low + size] * SCALE_LOG2 - top)
                mass = mass + jnp.sum(part.reshape(-1, 8, width), axis=0)
                weights[0, low:low + size] = part.astype(BF16)
            stats[slot, 0, head, pl.ds(block, 1)] = top
            stats[slot, 1, head, pl.ds(block, 1)] = jnp.sum(mass, axis=0, keepdims=True)


def in_parts(value):
    high = value.astype(BF16).astype(F32)
    middle = (value - high).astype(BF16).astype(F32)
    return [high, middle, value - high - middle]


def note_rows(peak, mass):
    rows = in_parts(peak) + in_parts(mass)
    index = lax.broadcasted_iota(jnp.int32, (NOTE_ROWS, peak.shape[1]), 0)
    result = jnp.zeros(index.shape, F32)
    for place, row in enumerate(rows):
        result = jnp.where(index == place, row, result)
    return result.astype(BF16)


def read_notes(notes):
    notes = notes.astype(F32)
    rows = [notes[place:place + 1] for place in range(6)]
    return rows[0] + rows[1] + rows[2], rows[3] + rows[4] + rows[5]


def slopes_kernel(owners, heads, blocks, slots, rows, who, counts, perm, stats, weights, values, keys_turned, *refs):
    pieces = refs[:2]
    slopes, turned, text_buf, sem = refs[-4:]
    step = pl.program_id(0)
    spans = spans_of(rows)
    chunks = text_buf.shape[1] // blocks
    width = chunks * HEAD_DIM
    tiles = own_tiles(owners, slots, who, counts, perm)

    @pl.when(step == 0)
    def _():
        for slot in range(slots):
            @pl.when(tiles[slot][0] < owners)
            def _(slot=slot):
                fetch(pieces, tiles[slot][0] ^ who[1], text_buf.at[slot], sem.at[slot])

    for slot in range(slots):
        base = slot * heads * blocks

        @pl.when((step == base) & (tiles[slot][0] < owners))
        def _(slot=slot):
            pltpu.make_async_copy(pieces[0].at[0], text_buf.at[slot], sem.at[slot]).wait()

        @pl.when((step >= base) & (step < base + heads * blocks) & (tiles[slot][0] < owners))
        def _(slot=slot, base=base):
            head, block = (step - base) // blocks, (step - base) % blocks
            grad = text_buf[slot, pl.ds(block * chunks, chunks), head, :HEAD_DIM].reshape(width, HEAD_DIM)
            delta = jnp.concatenate(
                [
                    text_buf[slot, block * chunks + piece, head, HEAD_DIM:].astype(F32)[:1]
                    for piece in range(chunks)
                ],
                axis=1,
            )
            for low, size, used in spans:
                slope = dot_nt(values[slot, low:low + size], grad)
                slopes[0, low:low + size] = (weights[0, low:low + size].astype(F32) * (slope - delta)).astype(BF16)
            total = dot_nn(keys_turned[slot, :, :slopes.shape[1]], slopes[0])
            columns = pl.ds(pl.multiple_of(block * width, width), width)
            turned[slot, head, :HEAD_DIM, columns] = total.astype(BF16)
            turned[slot, head, HEAD_DIM:, columns] = note_rows(
                stats[slot, 0, head, pl.ds(block, 1)], stats[slot, 1, head, pl.ds(block, 1)]
            )


def peak_and_mass(stats, owners, me, perm, start, tiles, head, block):
    found = []
    for index in range(MAX_TILES):
        live = index < tiles
        place = jnp.where(live, start + index, start)
        other, slot = perm[place & (owners - 1)] ^ me, lax.div(place, owners)
        top = stats[other, slot, 0, head, pl.ds(block, 1)]
        mass = stats[other, slot, 1, head, pl.ds(block, 1)]
        found.append((jnp.where(live, top, -jnp.inf), jnp.where(live, mass, 0.0)))
    top = functools.reduce(jnp.maximum, [peak for peak, _ in found])
    return top, sum(mass * jnp.exp2(peak - top) for peak, mass in found)


def factors_kernel(owners, heads, blocks, slots, who, counts, perm, *refs):
    out, stats = refs[-2:]
    for index, ref in enumerate(refs[:-2]):
        stats[2 * index:2 * index + 2] = ref[...]
    for slot, (sample, start) in enumerate(own_tiles(owners, slots, who, counts, perm)):
        @pl.when(sample < owners)
        def _(slot=slot, sample=sample, start=start):
            tiles = counts[jnp.minimum(sample, owners - 1)]
            for head in range(heads):
                for block in range(blocks):
                    top, mass = peak_and_mass(stats, owners, who[1], perm, start, tiles, head, block)
                    peak = stats[0, slot, 0, head, pl.ds(block, 1)]
                    out[slot, head, pl.ds(block, 1)] = jnp.exp2(peak - top) / mass


def sums_kernel(owners, heads, blocks, slots, slot, who, counts, perm, *refs):
    weights, slopes, factors = refs[:3]
    q_pieces, g_pieces = refs[3:5], refs[5:7]
    keep_out, send_out, q_buf, g_buf, sums, sem = refs[-6:]
    step = pl.program_id(0)
    odd, me = who[0] & 1, who[1]
    chunks = q_buf.shape[0] // blocks
    width = chunks * HEAD_DIM
    sample = own_tiles(owners, slots, who, counts, perm)[slot][0]
    used = sample < owners

    @pl.when((step == 0) & used)
    def _():
        fetch(q_pieces, sample ^ me, q_buf, sem.at[0])
        fetch(g_pieces, sample ^ me, g_buf, sem.at[1])
        pltpu.make_async_copy(q_pieces[0].at[0], q_buf, sem.at[0]).wait()
        pltpu.make_async_copy(g_pieces[0].at[0], g_buf, sem.at[1]).wait()

    @pl.when(jnp.logical_not(used))
    def _():
        keep_out[...] = jnp.zeros(keep_out.shape, BF16)
        send_out[...] = jnp.zeros(send_out.shape, BF16)

    @pl.when(used)
    def _():
        head, block = step // blocks, step % blocks
        factor = jnp.transpose(jnp.broadcast_to(factors[slot, head, pl.ds(block, 1)], (HEAD_DIM, width)))
        where = pl.ds(block * chunks, chunks)
        query = q_buf[where, head].reshape(width, HEAD_DIM)
        grad = g_buf[where, head, :HEAD_DIM].reshape(width, HEAD_DIM)
        query = (query.astype(F32) * factor * SCALE).astype(BF16)
        grad = (grad.astype(F32) * factor).astype(BF16)

        def add(which, source, right, fresh):
            for low in range(0, sums.shape[1], 2 * KEY_ROWS):
                span = slice(low, min(low + 2 * KEY_ROWS, sums.shape[1]))
                part = dot_nn(source[0, span], right)
                sums[which, span] = part if fresh else sums[which, span] + part

        for fresh in (True, False):
            @pl.when((step == 0) == fresh)
            def _(fresh=fresh):
                add(0, slopes, query, fresh)
                add(1, weights, grad, fresh)

        @pl.when(step == heads * blocks - 1)
        def _():
            keep_out[...] = sums[odd].astype(BF16)
            send_out[...] = sums[1 - odd].astype(BF16)


def route_kernel(owners, heads, blocks, slots, who, counts, perm, own, other, *refs):
    outs = refs[-(owners // 2):]
    me = who[1]
    width = own.shape[3] // blocks
    found = []
    for near in range(2):
        first = place_of(perm, me ^ near, owners)
        for slot in range(slots):
            found.append((near, slot, sample_at(counts, first + slot * owners, owners)[0]))

    def one(step, carry):
        head, block = step // blocks, step % blocks
        columns = pl.ds(pl.multiple_of(block * width, width), width)
        notes = [read_notes((own, other)[near][slot, head, HEAD_DIM:, columns]) for near, slot, _ in found]
        for distance, out in enumerate(outs):
            live = [sample == me ^ (2 * distance) for _, _, sample in found]
            top = functools.reduce(
                jnp.maximum, [jnp.where(hit, note[0], LOWEST) for hit, note in zip(live, notes)]
            )
            mass = jnp.zeros(top.shape, F32)
            total = jnp.zeros((HEAD_DIM, width), F32)
            for hit, note, (near, slot, _) in zip(live, notes, found):
                factor = jnp.exp2(jnp.where(hit, note[0] - top, -jnp.inf))
                mass = mass + jnp.where(hit, note[1] * factor, 0.0)
                part = (own, other)[near][slot, head, :HEAD_DIM, columns].astype(F32)
                total = total + jnp.where(hit, part * factor, 0.0)
            out[head, :HEAD_DIM, columns] = total.astype(BF16)
            out[head, HEAD_DIM:, columns] = note_rows(top, mass)
        return carry

    lax.fori_loop(0, heads * blocks, one, 0)


def gather_kernel(parts, *refs):
    outs = refs[parts:]
    rows = outs[0].shape[0]
    for piece, out in enumerate(outs):
        span = slice(piece * rows, (piece + 1) * rows)
        for head in range(refs[0].shape[0]):
            notes = [read_notes(ref[head, HEAD_DIM:, span]) for ref in refs[:parts]]
            top = functools.reduce(jnp.maximum, [note[0] for note in notes])
            factors = [jnp.exp2(note[0] - top) for note in notes]
            mass = sum(note[1] * factor for note, factor in zip(notes, factors))
            total = sum(ref[head, :HEAD_DIM, span].astype(F32) * factor for ref, factor in zip(refs[:parts], factors))
            total = total * (SCALE / mass)
            out[:, head * HEAD_DIM:(head + 1) * HEAD_DIM] = jnp.transpose(total).astype(BF16)


def place_kernel(who, *refs):
    out = refs[-1]
    for distance, ref in enumerate(refs[:-1]):
        width = ref.shape[1]
        start = pl.multiple_of((who[0] ^ distance) * width, width)
        out[:, pl.ds(start, width)] = ref[...]


def merge_kernel(slots, *refs):
    keep, got, out = refs[:slots], refs[slots:-1], refs[-1]
    for low, size, used in spans_of(out.shape[0]):
        row = lax.broadcasted_iota(jnp.int32, (slots * size, slots * size), 0)
        column = lax.broadcasted_iota(jnp.int32, (slots * size, slots * size), 1)
        source = lax.rem(row, slots) * size + lax.div(row, slots)
        order = (source == column).astype(BF16)
        total = [
            (keep[slot][low:low + size].astype(F32) + got[slot][low:low + size].astype(F32)).astype(BF16)
            for slot in range(slots)
        ]
        mixed = dot_nn(order, jnp.concatenate(total, axis=0)).astype(BF16).reshape(size, slots, HEAD_DIM)
        out[low:low + used] = mixed[:used]


def shards(queries, saved_output, grad_out, tile_kv, tile_count, owner_perm, text_len):
    rows_dev, features = queries.shape[1], queries.shape[2]
    groups, owners = lax.axis_size("seq"), lax.axis_size("dp")
    heads = features // HEAD_DIM // groups
    width = heads * HEAD_DIM
    chunks = min(TEXT_CHUNKS, groups)
    blocks = groups // chunks
    text_rows, block_rows = groups * rows_dev, chunks * rows_dev
    steps = heads * blocks
    slots, tile_rows = tile_kv.shape[0], tile_kv.shape[1]
    low, tail_rows, _ = spans_of(tile_rows)[-1]
    padded = low + tail_rows
    who = jnp.stack([lax.axis_index("seq"), lax.axis_index("dp")]).astype(jnp.int32)
    known = (who, tile_count, owner_perm)
    scale = blocks

    piece_rows = 2 * rows_dev + DELTA_ROWS
    packed = call(
        functools.partial(pack_kernel, heads),
        [jax.ShapeDtypeStruct((heads, piece_rows, HEAD_DIM), BF16)] * groups,
        [SMEM, SMEM] + [HBM] * 3,
        [pltpu.VMEM((rows_dev, features), BF16)] * 3 + [pltpu.SemaphoreType.DMA((3,))],
        (who, text_len, queries[0], saved_output[0], grad_out[0]),
        megabytes=60,
        cost=1,
    )
    pieces = [packed[0]] + [exchange(packed[j], "seq", j) for j in range(1, groups)]
    tile_shape = jax.ShapeDtypeStruct((slots, padded, HEAD_DIM), BF16)
    own_tile = call(pad_kernel, tile_shape, [VMEM] + [ANY] * (groups - 1), [], (tile_kv, *pieces[1:]), cost=1)
    partner_tile = exchange(own_tile, "seq", 1)

    def near_of(first, count, order):
        block = call(
            functools.partial(stack_kernel, groups, slice(first, first + count)),
            jax.ShapeDtypeStruct((groups, heads, count, HEAD_DIM), BF16),
            [ANY] * (groups + len(order)),
            [pltpu.SemaphoreType.DMA((groups,))],
            (*pieces, *order),
            megabytes=8,
        )
        return [block] + [exchange(block, "dp", d) for d in range(2, owners, 2)]

    def over_core(near, order):
        joined = call(
            functools.partial(join_kernel, len(near)),
            jax.ShapeDtypeStruct((len(near),) + near[0].shape, BF16),
            [ANY] * (len(near) + len(order)),
            [pltpu.SemaphoreType.DMA((len(near),))],
            (*near, *order),
            megabytes=12 * scale,
        )
        return joined, exchange(joined, "dp", 1)

    q_near = near_of(0, rows_dev, [own_tile])
    g_near = near_of(rows_dev, rows_dev + DELTA_ROWS, q_near[1:2])
    q_pair = over_core(q_near, [partner_tile])

    turn_shape = jax.ShapeDtypeStruct((slots, HEAD_DIM, -(-padded // HEAD_DIM) * HEAD_DIM), BF16)
    keys, values, keys_turned = call(
        functools.partial(tiles_kernel, slots, tile_rows),
        [tile_shape, tile_shape, turn_shape],
        [SMEM] + [VMEM] * 2,
        [],
        (who, own_tile, partner_tile),
        cost=1,
    )
    stats_shape = (slots, 2, heads, blocks, block_rows)
    stack_shape = jax.ShapeDtypeStruct((slots * steps, padded, block_rows), BF16)
    stack_spec = pl.BlockSpec((1, padded, block_rows), lambda i: (i, 0, 0))
    stats, weights = call(
        functools.partial(weights_kernel, owners, heads, blocks, slots, tile_rows),
        [jax.ShapeDtypeStruct(stats_shape, F32), stack_shape],
        [SMEM] * 3 + [VMEM] + [ANY] * 2,
        [
            pltpu.VMEM((slots,) + q_near[0].shape, BF16),
            pltpu.VMEM((padded, block_rows), F32),
            pltpu.SemaphoreType.DMA((slots,)),
        ],
        (*known, keys, *q_pair),
        out_specs=[VMEM, stack_spec],
        grid=(slots * steps,),
        megabytes=16,
        cost=6,
    )
    pair = jnp.stack([stats, exchange(stats, "dp", 1)])
    shared = [pair] + [exchange(pair, "dp", d) for d in range(2, owners, 2)]
    g_pair = over_core(g_near, [stats])
    slopes, part = call(
        functools.partial(slopes_kernel, owners, heads, blocks, slots, tile_rows),
        [stack_shape, jax.ShapeDtypeStruct((slots, heads, HEAD_DIM + NOTE_ROWS, text_rows), BF16)],
        [SMEM] * 3 + [VMEM, stack_spec] + [VMEM] * 2 + [ANY] * 3,
        [pltpu.VMEM((slots,) + g_near[0].shape, BF16), pltpu.SemaphoreType.DMA((slots,))],
        (*known, stats, weights, values, keys_turned, *g_pair, pair),
        out_specs=[stack_spec, VMEM],
        grid=(slots * steps,),
        megabytes=20,
        cost=6,
    )
    factors = call(
        functools.partial(factors_kernel, owners, heads, blocks, slots),
        jax.ShapeDtypeStruct((slots, heads, blocks, block_rows), F32),
        [SMEM] * 3 + [VMEM] * len(shared),
        [pltpu.VMEM((owners,) + stats_shape, F32)],
        (*known, *shared),
        cost=30,
    )
    routed = call(
        functools.partial(route_kernel, owners, heads, blocks, slots),
        [jax.ShapeDtypeStruct((heads, HEAD_DIM + NOTE_ROWS, text_rows), BF16)] * (owners // 2),
        [SMEM] * 3 + [VMEM] * 2 + [ANY],
        [],
        (*known, part, exchange(part, "dp", 1), factors),
        megabytes=14,
        cost=30,
    )

    kept, got = [], []
    for slot in range(slots):
        left_spec = pl.BlockSpec((1, padded, block_rows), lambda i, slot=slot: (slot * steps + i, 0, 0))
        keep, send = call(
            functools.partial(sums_kernel, owners, heads, blocks, slots, slot),
            [jax.ShapeDtypeStruct((padded, HEAD_DIM), BF16)] * 2,
            [SMEM] * 3 + [left_spec] * 2 + [VMEM] + [ANY] * 5,
            [
                pltpu.VMEM(q_near[0].shape, BF16),
                pltpu.VMEM(g_near[0].shape, BF16),
                pltpu.VMEM((2, padded, HEAD_DIM), F32),
                pltpu.SemaphoreType.DMA((2,)),
            ],
            (*known, weights, slopes, factors, *q_pair, *g_pair, routed[0]),
            out_specs=[VMEM] * 2,
            grid=(steps,),
            megabytes=8 * scale,
            cost=4,
        )
        kept.append(keep)
        got.append(exchange(send, "seq", 1))

    sums = [routed[0]] + [exchange(routed[d], "dp", 2 * d) for d in range(1, owners // 2)]
    cut = call(
        functools.partial(gather_kernel, len(sums)),
        [jax.ShapeDtypeStruct((rows_dev, width), BF16)] * groups,
        [VMEM] * len(sums),
        [],
        sums,
        megabytes=8 * scale,
        cost=30,
    )
    back = [cut[0]] + [exchange(cut[j], "seq", j) for j in range(1, groups)]
    grad_queries = call(
        place_kernel,
        jax.ShapeDtypeStruct((rows_dev, features), BF16),
        [SMEM] + [VMEM] * groups,
        [],
        (who, *back),
        cost=1,
    )
    grad_tiles = call(
        functools.partial(merge_kernel, slots),
        jax.ShapeDtypeStruct((tile_rows, slots, HEAD_DIM), BF16),
        [VMEM] * (2 * slots),
        [],
        (*kept, *got),
        cost=2,
    )
    return (grad_queries[None], jnp.transpose(grad_tiles, (1, 0, 2)))


def solution(mesh):
    placed = (
        P("dp", "seq", None),
        P("dp", "seq", None),
        P("dp", "seq", None),
        P("dp", None, "seq"),
        P(),
        P(),
        P("dp"),
    )
    return jax.shard_map(
        shards,
        mesh=mesh,
        in_specs=placed,
        out_specs=(P("dp", "seq", None), P("dp", None, "seq")),
        check_vma=False,
    )
```

```python
import functools
import math

import jax
import jax.numpy as jnp
from jax import lax
from jax.experimental import pallas as pl
from jax.experimental.pallas import tpu as pltpu
from jax.sharding import PartitionSpec as P

HEAD_DIM = 128
MAX_TILES = 4
KEY_ROWS = 256
TEXT_CHUNKS = 4
TILE = 16
TERMS = 6
LOWEST = -1e30
SCALE = 1.0 / math.sqrt(HEAD_DIM)
SCALE_LOG2 = SCALE / math.log(2.0)
BF16 = jnp.bfloat16
F32 = jnp.float32

SMEM = pl.BlockSpec(memory_space=pltpu.SMEM)
VMEM = pl.BlockSpec(memory_space=pltpu.VMEM)
ANY = pl.BlockSpec(memory_space=pl.ANY)
HBM = pl.BlockSpec(memory_space=pltpu.HBM)


def whole_tiles(rows):
    return -(-rows // TILE) * TILE


def exchange(block, axis, distance):
    count = lax.axis_size(axis)
    return lax.ppermute(block, axis, [(i, i ^ distance) for i in range(count)])


def call(kernel, out_shape, in_specs, scratch, args, out_specs=None, grid=(), megabytes=16, cost=0):
    many = isinstance(out_shape, (list, tuple))
    if out_specs is None:
        out_specs = [VMEM] * len(out_shape) if many else VMEM
    return pl.pallas_call(
        kernel,
        out_shape=out_shape,
        in_specs=in_specs,
        out_specs=out_specs,
        grid=grid,
        name=getattr(kernel, "func", kernel).__name__,
        scratch_shapes=scratch,
        compiler_params=pltpu.CompilerParams(vmem_limit_bytes=megabytes << 20),
        cost_estimate=pl.CostEstimate(flops=cost * 10**9, bytes_accessed=0, transcendentals=0),
    )(*args)


def place_of(perm_ref, owner, owners):
    first = jnp.int32(0)
    for index in range(owners):
        first = first + jnp.where(perm_ref[index] == owner, index, 0)
    return first


def sample_at(count_ref, place, samples):
    end, sample, start = jnp.int32(0), jnp.int32(0), jnp.int32(0)
    for index in range(samples):
        end = end + count_ref[index]
        passed = place >= end
        sample = sample + passed.astype(jnp.int32)
        start = jnp.where(passed, end, start)
    return sample, start


def pack_kernel(heads, who, length, *refs):
    inputs, outs, buffers, sem = refs[:3], refs[3:-4], refs[-4:-1], refs[-1]
    copies = [pltpu.make_async_copy(a, b, sem.at[i]) for i, (a, b) in enumerate(zip(inputs, buffers))]
    for copy in copies:
        copy.start()
    for copy in copies:
        copy.wait()
    q_ref, o_ref, g_ref = buffers
    rows = q_ref.shape[0]
    seq = who[0]
    position = seq * rows + lax.broadcasted_iota(jnp.int32, (rows, HEAD_DIM), 0)
    keep = position < length[0]
    for j, out in enumerate(outs):
        place = lax.broadcasted_iota(jnp.int32, (out.shape[0] - 2 * heads * rows, HEAD_DIM), 0)
        deltas = jnp.zeros(place.shape, F32)
        for h in range(heads):
            columns = pl.ds(pl.multiple_of(((seq ^ j) * heads + h) * HEAD_DIM, HEAD_DIM), HEAD_DIM)
            grad = jnp.where(keep, g_ref[:, columns].astype(F32), 0.0)
            product = grad * o_ref[:, columns].astype(F32)
            delta = jnp.sum(jnp.transpose(product), axis=0, keepdims=True)
            out[h * rows:(h + 1) * rows] = q_ref[:, columns]
            out[(heads + h) * rows:(heads + h + 1) * rows] = grad.astype(BF16)
            deltas = jnp.where(place == j * heads + h, delta, deltas)
        out[2 * heads * rows:] = deltas.astype(BF16)


def stack_kernel(count, rows, extra, *refs):
    out, buffer, sem = refs[-3:]
    size = rows.stop - rows.start
    copies = [
        pltpu.make_async_copy(refs[i].at[rows], out.at[pl.ds(i * size, size)], sem.at[0, i]) for i in range(count)
    ]
    if extra:
        last = pl.ds(refs[0].shape[0] - extra, extra)
        copies += [pltpu.make_async_copy(refs[i].at[last], buffer.at[i], sem.at[1, i]) for i in range(count)]
    for copy in copies:
        copy.start()
    for copy in copies:
        copy.wait()
    if extra:
        out[count * size:] = sum(buffer[i].astype(F32) for i in range(count)).astype(BF16)


def join_kernel(count, *refs):
    out, sem = refs[-2], refs[-1]
    first = refs[0].shape[0]
    copies = []
    for i in range(count):
        second = refs[count + i].shape[0]
        copies.append(pltpu.make_async_copy(refs[i], out.at[i, pl.ds(0, first)], sem.at[0, i]))
        copies.append(pltpu.make_async_copy(refs[count + i], out.at[i, pl.ds(first, second)], sem.at[1, i]))
    for copy in copies:
        copy.start()
    for copy in copies:
        copy.wait()


def fetch(pieces, relative, target, sem):
    for distance, piece in enumerate(pieces):
        @pl.when(relative == distance)
        def _(piece=piece):
            pltpu.make_async_copy(piece, target, sem).start()


def fetch_pair(pieces, relative, target, sem):
    rows = pl.ds(0, target.shape[0])
    for core, piece in enumerate(pieces):
        @pl.when((relative & 1) == core)
        def _(piece=piece):
            pltpu.make_async_copy(piece.at[lax.shift_right_logical(relative, 1), rows], target, sem).start()


def spans_of(rows):
    full = rows // KEY_ROWS
    tail = rows - full * KEY_ROWS
    return [(i * KEY_ROWS, KEY_ROWS, KEY_ROWS) for i in range(full)] + [(full * KEY_ROWS, -(-tail // 16) * 16, tail)]


def dot_nt(a, b):
    return lax.dot_general(a, b, (((1,), (1,)), ((), ())), preferred_element_type=F32)


def dot_nn(a, b):
    return jnp.dot(a, b, preferred_element_type=F32)


def own_tiles(owners, slots, who, counts, perm):
    first = place_of(perm, who[1], owners)
    return [sample_at(counts, first + slot * owners, owners) for slot in range(slots)]


def pad_kernel(tiles, *refs):
    out = refs[-1]
    for slot in range(tiles.shape[0]):
        for low, size, used in spans_of(tiles.shape[1]):
            if size != used:
                out[slot, low:] = jnp.zeros((size, HEAD_DIM), BF16)
            out[slot, low:low + used] = tiles[slot, low:low + used]


def tiles_kernel(slots, rows, who, own, partner, keys, values, turned):
    for odd in range(2):
        @pl.when((who[0] & 1) == odd)
        def _(odd=odd):
            keys[...] = (own, partner)[odd][...]
            values[...] = (own, partner)[1 - odd][...]
    for slot in range(slots):
        for low, size, _ in spans_of(rows):
            turned[slot, :, low:low + size] = jnp.transpose(keys[slot, low:low + size].astype(F32)).astype(BF16)


def weights_kernel(owners, heads, blocks, slots, rows, who, counts, perm, keys, *refs):
    pieces = refs[:owners]
    notes, weights, text_buf, scores_buf, stats, sem = refs[owners:]
    step = pl.program_id(0)
    spans = spans_of(rows)
    groups = text_buf.shape[1] // (heads * HEAD_DIM)
    chunks = groups // blocks
    width = chunks * HEAD_DIM
    tiles = own_tiles(owners, slots, who, counts, perm)

    @pl.when(step == 0)
    def _():
        for slot in range(slots):
            @pl.when(tiles[slot][0] < owners)
            def _(slot=slot):
                fetch(pieces, tiles[slot][0] ^ who[1], text_buf.at[slot], sem.at[slot])

    for slot in range(slots):
        base = slot * heads * blocks

        @pl.when((step == base) & (tiles[slot][0] < owners))
        def _(slot=slot):
            pltpu.make_async_copy(pieces[0], text_buf.at[slot], sem.at[slot]).wait()

        @pl.when((step >= base) & (step < base + heads * blocks) & (tiles[slot][0] < owners))
        def _(slot=slot, base=base):
            head, block = (step - base) // blocks, (step - base) % blocks
            query = rows_of(text_buf.at[slot], heads, head, block, chunks)
            peak = jnp.full((8, width), -jnp.inf, F32)
            for low, size, used in spans:
                scores = dot_nt(keys[slot, low:low + size], query)
                if size != used:
                    row = lax.broadcasted_iota(jnp.int32, scores.shape, 0)
                    scores = jnp.where(row < used, scores, -jnp.inf)
                scores_buf[low:low + size] = scores
                peak = jnp.maximum(peak, jnp.max(scores.reshape(-1, 8, width), axis=0))
            top = jnp.max(peak, axis=0, keepdims=True) * SCALE_LOG2
            mass = jnp.zeros((8, width), F32)
            for low, size, used in spans:
                part = jnp.exp2(scores_buf[low:low + size] * SCALE_LOG2 - top)
                mass = mass + jnp.sum(part.reshape(-1, 8, width), axis=0)
                weights[0, low:low + size] = part.astype(BF16)
            stats[2 * head, pl.ds(block, 1)] = top
            stats[2 * head + 1, pl.ds(block, 1)] = jnp.sum(mass, axis=0, keepdims=True)

            @pl.when(step == base + heads * blocks - 1)
            def _():
                for done in range(blocks):
                    lines = [stats[index, done:done + 1] for index in range(2 * heads)]
                    full = note_rows(lines)
                    size = full.shape[0]
                    for chunk in range(chunks):
                        first = (slot * groups + done * chunks + chunk) * size
                        notes[first:first + size] = full[:, chunk * HEAD_DIM:(chunk + 1) * HEAD_DIM]


def in_parts(value):
    high = value.astype(BF16).astype(F32)
    middle = (value - high).astype(BF16).astype(F32)
    return [high, middle, value - high - middle]


def note_rows(lines):
    rows = [term for line in lines for term in in_parts(line)]
    index = lax.broadcasted_iota(jnp.int32, (whole_tiles(len(rows)), lines[0].shape[1]), 0)
    result = jnp.zeros(index.shape, F32)
    for place, row in enumerate(rows):
        result = jnp.where(index == place, row, result)
    return result.astype(BF16)


def read_notes(notes, head):
    notes = notes.astype(F32)
    rows = [notes[place:place + 1] for place in range(TERMS * head, TERMS * head + TERMS)]
    return rows[0] + rows[1] + rows[2], rows[3] + rows[4] + rows[5]


def rows_of(text, heads, head, block, chunks):
    first = block * chunks * heads + head
    starts = [pl.multiple_of((first + chunk * heads) * HEAD_DIM, HEAD_DIM) for chunk in range(chunks)]
    return jnp.concatenate([text[pl.ds(start, HEAD_DIM)] for start in starts], axis=0)


def slopes_kernel(owners, heads, blocks, slots, rows, who, counts, perm, notes, weights, values, keys_turned, *refs):
    pieces = refs[:2]
    slopes, turned, text_buf, deltas, sem = refs[-5:]
    step = pl.program_id(0)
    spans = spans_of(rows)
    groups = turned.shape[2] // HEAD_DIM
    chunks = groups // blocks
    text_rows = groups * heads * HEAD_DIM
    width = chunks * HEAD_DIM
    tiles = own_tiles(owners, slots, who, counts, perm)

    @pl.when(step == 0)
    def _():
        for slot in range(slots):
            @pl.when(tiles[slot][0] < owners)
            def _(slot=slot):
                fetch_pair(pieces, tiles[slot][0] ^ who[1], text_buf.at[slot], sem.at[slot])

            @pl.when(tiles[slot][0] >= owners)
            def _(slot=slot):
                turned[slot] = jnp.zeros(turned.shape[1:], BF16)

    for slot in range(slots):
        base = slot * heads * blocks

        @pl.when((step == base) & (tiles[slot][0] < owners))
        def _(slot=slot):
            pltpu.make_async_copy(pieces[0].at[0, pl.ds(0, text_buf.shape[1])], text_buf.at[slot], sem.at[slot]).wait()
            deltas[...] = text_buf[slot, text_rows:].astype(F32)
            size = turned.shape[1] - heads * HEAD_DIM
            for chunk in range(groups):
                first = (slot * groups + chunk) * size
                columns = slice(chunk * HEAD_DIM, (chunk + 1) * HEAD_DIM)
                turned[slot, heads * HEAD_DIM:, columns] = notes[first:first + size]

        @pl.when((step >= base) & (step < base + heads * blocks) & (tiles[slot][0] < owners))
        def _(slot=slot, base=base):
            head, block = (step - base) // blocks, (step - base) % blocks
            grad = rows_of(text_buf.at[slot], heads, head, block, chunks)
            first = block * chunks * heads + head
            delta = jnp.concatenate([deltas[pl.ds(first + chunk * heads, 1)] for chunk in range(chunks)], axis=1)
            for low, size, used in spans:
                slope = dot_nt(values[slot, low:low + size], grad)
                slopes[0, low:low + size] = (weights[0, low:low + size].astype(F32) * (slope - delta)).astype(BF16)
            total = dot_nn(keys_turned[slot, :, :slopes.shape[1]], slopes[0])
            columns = pl.ds(pl.multiple_of(block * width, width), width)
            turned[slot, pl.ds(pl.multiple_of(head * HEAD_DIM, HEAD_DIM), HEAD_DIM), columns] = total.astype(BF16)


def peak_and_mass(notes, owners, heads, groups, me, perm, start, tiles, head, chunk):
    found = []
    size = whole_tiles(TERMS * heads)
    for index in range(MAX_TILES):
        live = index < tiles
        place = jnp.where(live, start + index, start)
        other, slot = perm[place & (owners - 1)] ^ me, lax.div(place, owners)
        first = pl.multiple_of((slot * groups + chunk) * size, size)
        top, mass = read_notes(notes[other, pl.ds(first, size)], head)
        found.append((jnp.where(live, top, -jnp.inf), jnp.where(live, mass, 0.0)))
    top = functools.reduce(jnp.maximum, [peak for peak, _ in found])
    return top, sum(mass * jnp.exp2(peak - top) for peak, mass in found)


def factors_kernel(owners, heads, groups, slots, who, counts, perm, own, other, out, notes, sem):
    copies = []
    rows = notes.shape[1]
    for core, source in enumerate((own, other)):
        for chip in range(owners // 2):
            place = 2 * chip + core
            part = source.at[chip, pl.ds(source.shape[1] - rows, rows)]
            copies.append(pltpu.make_async_copy(part, notes.at[place], sem.at[place]))
    for copy in copies:
        copy.start()
    for copy in copies:
        copy.wait()
    size = whole_tiles(TERMS * heads)
    for slot, (sample, start) in enumerate(own_tiles(owners, slots, who, counts, perm)):
        @pl.when(sample < owners)
        def _(slot=slot, sample=sample, start=start):
            tiles = counts[jnp.minimum(sample, owners - 1)]
            for head in range(heads):
                for chunk in range(groups):
                    top, mass = peak_and_mass(
                        notes, owners, heads, groups, who[1], perm, start, tiles, head, chunk
                    )
                    first = (slot * groups + chunk) * size
                    peak = read_notes(notes[0, first:first + size], head)[0]
                    out[slot, head, chunk:chunk + 1] = jnp.exp2(peak - top) / mass


def sums_kernel(owners, heads, blocks, slots, slot, who, counts, perm, *refs):
    weights, slopes, factors = refs[:3]
    q_pieces, g_pieces = refs[3:3 + owners], refs[3 + owners:5 + owners]
    keep_out, send_out, q_buf, g_buf, sums, sem = refs[-6:]
    step = pl.program_id(0)
    odd, me = who[0] & 1, who[1]
    groups = q_buf.shape[0] // (heads * HEAD_DIM)
    chunks = groups // blocks
    width = chunks * HEAD_DIM
    sample = own_tiles(owners, slots, who, counts, perm)[slot][0]
    used = sample < owners

    @pl.when((step == 0) & used)
    def _():
        fetch(q_pieces, sample ^ me, q_buf, sem.at[0])
        fetch_pair(g_pieces, sample ^ me, g_buf, sem.at[1])
        pltpu.make_async_copy(q_pieces[0], q_buf, sem.at[0]).wait()
        pltpu.make_async_copy(g_pieces[0].at[0, pl.ds(0, g_buf.shape[0])], g_buf, sem.at[1]).wait()

    @pl.when(jnp.logical_not(used))
    def _():
        keep_out[...] = jnp.zeros(keep_out.shape, BF16)
        send_out[...] = jnp.zeros(send_out.shape, BF16)

    @pl.when(used)
    def _():
        head, block = step // blocks, step % blocks
        factor = jnp.concatenate(
            [factors[slot, head, pl.ds(block * chunks + chunk, 1)] for chunk in range(chunks)], axis=1
        )
        factor = jnp.transpose(jnp.broadcast_to(factor, (HEAD_DIM, width)))
        query = rows_of(q_buf, heads, head, block, chunks)
        grad = rows_of(g_buf, heads, head, block, chunks)
        query = (query.astype(F32) * factor * SCALE).astype(BF16)
        grad = (grad.astype(F32) * factor).astype(BF16)

        def add(which, source, right, fresh):
            for low in range(0, sums.shape[1], 2 * KEY_ROWS):
                span = slice(low, min(low + 2 * KEY_ROWS, sums.shape[1]))
                part = dot_nn(source[0, span], right)
                sums[which, span] = part if fresh else sums[which, span] + part

        for fresh in (True, False):
            @pl.when((step == 0) == fresh)
            def _(fresh=fresh):
                add(0, slopes, query, fresh)
                add(1, weights, grad, fresh)

        @pl.when(step == heads * blocks - 1)
        def _():
            keep_out[...] = sums[odd].astype(BF16)
            send_out[...] = sums[1 - odd].astype(BF16)


def route_kernel(owners, heads, blocks, slots, who, counts, perm, own, other, *refs):
    outs = refs[-(owners // 2):]
    me = who[1]
    width = own.shape[2] // blocks
    split = heads * HEAD_DIM
    found = []
    for near in range(2):
        first = place_of(perm, me ^ near, owners)
        for slot in range(slots):
            found.append((near, slot, sample_at(counts, first + slot * owners, owners)[0]))

    def one(block, carry):
        columns = pl.ds(pl.multiple_of(block * width, width), width)
        sources = [(own, other)[near].at[slot] for near, slot, _ in found]
        notes = [source[split:, columns] for source in sources]
        lines = [[] for _ in outs]
        for head in range(heads):
            rows = slice(head * HEAD_DIM, (head + 1) * HEAD_DIM)
            parts = [source[rows, columns].astype(F32) for source in sources]
            known = [read_notes(note, head) for note in notes]
            for distance, out in enumerate(outs):
                live = [sample == me ^ (2 * distance) for _, _, sample in found]
                tops = [jnp.where(hit, note[0], LOWEST) for hit, note in zip(live, known)]
                top = functools.reduce(jnp.maximum, tops)
                factors = [jnp.where(hit, jnp.exp2(peak - top), 0.0) for hit, peak in zip(live, tops)]
                mass = sum(note[1] * factor for note, factor in zip(known, factors))
                out[rows, columns] = sum(part * factor for part, factor in zip(parts, factors)).astype(BF16)
                lines[distance] += [top, mass]
        for distance, out in enumerate(outs):
            out[split:, columns] = note_rows(lines[distance])
        return carry

    lax.fori_loop(0, blocks, one, 0)


def gather_kernel(heads, parts, *refs):
    outs = refs[parts:]
    rows = outs[0].shape[0]
    split = heads * HEAD_DIM
    for piece, out in enumerate(outs):
        span = slice(piece * rows, (piece + 1) * rows)
        blocks = [ref[split:, span] for ref in refs[:parts]]
        for head in range(heads):
            lanes = slice(head * HEAD_DIM, (head + 1) * HEAD_DIM)
            notes = [read_notes(block, head) for block in blocks]
            top = functools.reduce(jnp.maximum, [note[0] for note in notes])
            factors = [jnp.exp2(note[0] - top) for note in notes]
            mass = sum(note[1] * factor for note, factor in zip(notes, factors))
            total = sum(ref[lanes, span].astype(F32) * factor for ref, factor in zip(refs[:parts], factors))
            out[:, lanes] = jnp.transpose(total * (SCALE / mass)).astype(BF16)


def place_kernel(who, *refs):
    out = refs[-1]
    for distance, ref in enumerate(refs[:-2]):
        width = ref.shape[1]
        start = pl.multiple_of((who[0] ^ distance) * width, width)
        out[:, pl.ds(start, width)] = ref[...]


def merge_kernel(slots, *refs):
    keep, got, out, done = refs[:slots], refs[slots:-2], refs[-2], refs[-1]
    done[...] = jnp.zeros(done.shape, BF16)
    for low, size, used in spans_of(out.shape[0]):
        row = lax.broadcasted_iota(jnp.int32, (slots * size, slots * size), 0)
        column = lax.broadcasted_iota(jnp.int32, (slots * size, slots * size), 1)
        source = lax.rem(row, slots) * size + lax.div(row, slots)
        order = (source == column).astype(BF16)
        total = [
            (keep[slot][low:low + size].astype(F32) + got[slot][low:low + size].astype(F32)).astype(BF16)
            for slot in range(slots)
        ]
        mixed = dot_nn(order, jnp.concatenate(total, axis=0)).astype(BF16).reshape(size, slots, HEAD_DIM)
        out[low:low + used] = mixed[:used]


def shards(queries, saved_output, grad_out, tile_kv, tile_count, owner_perm, text_len):
    rows_dev, features = queries.shape[1], queries.shape[2]
    groups, owners = lax.axis_size("seq"), lax.axis_size("dp")
    heads = features // HEAD_DIM // groups
    width = heads * HEAD_DIM
    chunks = min(TEXT_CHUNKS, groups)
    blocks = groups // chunks
    text_rows, block_rows = groups * rows_dev, chunks * rows_dev
    steps = heads * blocks
    slots, tile_rows = tile_kv.shape[0], tile_kv.shape[1]
    low, tail_rows, _ = spans_of(tile_rows)[-1]
    padded = low + tail_rows
    who = jnp.stack([lax.axis_index("seq"), lax.axis_index("dp")]).astype(jnp.int32)
    known = (who, tile_count, owner_perm)
    scale = blocks

    delta_rows = whole_tiles(groups * heads)
    piece_rows = 2 * heads * rows_dev + delta_rows
    note_size = whole_tiles(TERMS * heads)
    note_count = slots * groups * note_size
    packed = call(
        functools.partial(pack_kernel, heads),
        [jax.ShapeDtypeStruct((piece_rows, HEAD_DIM), BF16)] * groups,
        [SMEM, SMEM] + [HBM] * 3,
        [pltpu.VMEM((rows_dev, features), BF16)] * 3 + [pltpu.SemaphoreType.DMA((3,))],
        (who, text_len, queries[0], saved_output[0], grad_out[0]),
        megabytes=16,
        cost=1,
    )
    pieces = [packed[0]] + [exchange(packed[j], "seq", j) for j in range(1, groups)]
    tile_shape = jax.ShapeDtypeStruct((slots, padded, HEAD_DIM), BF16)
    own_tile = call(pad_kernel, tile_shape, [VMEM] + [ANY] * (groups - 1), [], (tile_kv, *pieces[1:]), cost=1)
    partner_tile = exchange(own_tile, "seq", 1)

    def near_of(first, extra, order):
        block = call(
            functools.partial(stack_kernel, groups, slice(first, first + heads * rows_dev), extra),
            jax.ShapeDtypeStruct((groups * heads * rows_dev + extra, HEAD_DIM), BF16),
            [HBM] + [ANY] * (groups - 1 + len(order)),
            [pltpu.VMEM((groups, delta_rows, HEAD_DIM), BF16), pltpu.SemaphoreType.DMA((2, groups))],
            (*pieces, *order),
            megabytes=8 * scale,
        )
        return near(block)

    def near(block):
        return [block] + [exchange(block, "dp", d) for d in range(2, owners, 2)]

    q_near = near_of(0, 0, [own_tile])
    g_near = near_of(heads * rows_dev, delta_rows, q_near[1:2])
    q_all = [block for piece in q_near for block in (piece, exchange(piece, "dp", 1))]

    turn_shape = jax.ShapeDtypeStruct((slots, HEAD_DIM, -(-padded // HEAD_DIM) * HEAD_DIM), BF16)
    keys, values, keys_turned = call(
        functools.partial(tiles_kernel, slots, tile_rows),
        [tile_shape, tile_shape, turn_shape],
        [SMEM] + [VMEM] * 2,
        [],
        (who, own_tile, partner_tile),
        cost=0,
    )
    stack_shape = jax.ShapeDtypeStruct((slots * steps, padded, block_rows), BF16)
    stack_spec = pl.BlockSpec((1, padded, block_rows), lambda i: (i, 0, 0))
    notes, weights = call(
        functools.partial(weights_kernel, owners, heads, blocks, slots, tile_rows),
        [jax.ShapeDtypeStruct((note_count, HEAD_DIM), BF16), stack_shape],
        [SMEM] * 3 + [VMEM] + [ANY] * owners,
        [
            pltpu.VMEM((slots,) + q_near[0].shape, BF16),
            pltpu.VMEM((padded, block_rows), F32),
            pltpu.VMEM((2 * heads, blocks, block_rows), F32),
            pltpu.SemaphoreType.DMA((slots,)),
        ],
        (*known, keys, *q_all),
        out_specs=[VMEM, stack_spec],
        grid=(slots * steps,),
        megabytes=16,
        cost=0,
    )
    notes_near = near(notes)
    joined = call(
        functools.partial(join_kernel, owners // 2),
        jax.ShapeDtypeStruct((owners // 2, g_near[0].shape[0] + note_count, HEAD_DIM), BF16),
        [ANY] * owners,
        [pltpu.SemaphoreType.DMA((2, owners // 2))],
        (*g_near, *notes_near),
        megabytes=12 * scale,
    )
    g_pair = (joined, exchange(joined, "dp", 1))
    slopes, part = call(
        functools.partial(slopes_kernel, owners, heads, blocks, slots, tile_rows),
        [stack_shape, jax.ShapeDtypeStruct((slots, width + note_size, text_rows), BF16)],
        [SMEM] * 3 + [VMEM, stack_spec] + [VMEM] * 2 + [ANY] * 2,
        [
            pltpu.VMEM((slots,) + g_near[0].shape, BF16),
            pltpu.VMEM((delta_rows, HEAD_DIM), F32),
            pltpu.SemaphoreType.DMA((slots,)),
        ],
        (*known, notes, weights, values, keys_turned, *g_pair),
        out_specs=[stack_spec, VMEM],
        grid=(slots * steps,),
        megabytes=20,
        cost=6,
    )
    factors = call(
        functools.partial(factors_kernel, owners, heads, groups, slots),
        jax.ShapeDtypeStruct((slots, heads, groups, HEAD_DIM), F32),
        [SMEM] * 3 + [ANY] * 2,
        [pltpu.VMEM((owners, note_count, HEAD_DIM), BF16), pltpu.SemaphoreType.DMA((owners,))],
        (*known, *g_pair),
        cost=30,
    )
    kept, got = [], []

    def tile_sums(slot, order):
        left_spec = pl.BlockSpec((1, padded, block_rows), lambda i: (slot * steps + i, 0, 0))
        keep, send = call(
            functools.partial(sums_kernel, owners, heads, blocks, slots, slot),
            [jax.ShapeDtypeStruct((padded, HEAD_DIM), BF16)] * 2,
            [SMEM] * 3 + [left_spec] * 2 + [VMEM] + [ANY] * (owners + 2 + len(order)),
            [
                pltpu.VMEM(q_near[0].shape, BF16),
                pltpu.VMEM(g_near[0].shape, BF16),
                pltpu.VMEM((2, padded, HEAD_DIM), F32),
                pltpu.SemaphoreType.DMA((2,)),
            ],
            (*known, weights, slopes, factors, *q_all, *g_pair, *order),
            out_specs=[VMEM] * 2,
            grid=(steps,),
            megabytes=8 * scale,
            cost=4,
        )
        kept.append(keep)
        got.append(exchange(send, "seq", 1))

    tile_sums(0, [])
    routed = call(
        functools.partial(route_kernel, owners, heads, blocks, slots),
        [jax.ShapeDtypeStruct((width + note_size, text_rows), BF16)] * (owners // 2),
        [SMEM] * 3 + [VMEM] * 2 + [ANY] * 2,
        [],
        (*known, part, exchange(part, "dp", 1), factors, kept[0]),
        megabytes=14,
        cost=30,
    )

    for slot in range(1, slots):
        tile_sums(slot, [routed[0]])

    sums = [routed[0]] + [exchange(routed[d], "dp", 2 * d) for d in range(1, owners // 2)]
    cut = call(
        functools.partial(gather_kernel, heads, len(sums)),
        [jax.ShapeDtypeStruct((rows_dev, width), BF16)] * groups,
        [VMEM] * len(sums),
        [],
        sums,
        megabytes=8 * scale,
        cost=30,
    )
    back = [cut[0]] + [exchange(cut[j], "seq", j) for j in range(1, groups)]
    grad_tiles, merged = call(
        functools.partial(merge_kernel, slots),
        [jax.ShapeDtypeStruct((tile_rows, slots, HEAD_DIM), BF16), jax.ShapeDtypeStruct((TILE, HEAD_DIM), BF16)],
        [VMEM] * (2 * slots),
        [],
        (*kept, *got),
        cost=2,
    )
    grad_queries = call(
        place_kernel,
        jax.ShapeDtypeStruct((rows_dev, features), BF16),
        [SMEM] + [VMEM] * groups + [ANY],
        [],
        (who, *back, merged),
        cost=1,
    )
    return (grad_queries[None], jnp.transpose(grad_tiles, (1, 0, 2)))


def solution(mesh):
    placed = (
        P("dp", "seq", None),
        P("dp", "seq", None),
        P("dp", "seq", None),
        P("dp", None, "seq"),
        P(),
        P(),
        P("dp"),
    )
    return jax.shard_map(
        shards,
        mesh=mesh,
        in_specs=placed,
        out_specs=(P("dp", "seq", None), P("dp", None, "seq")),
        check_vma=False,
    )
```

```python
import functools
import math

import jax
import jax.numpy as jnp
from jax import lax
from jax.experimental import pallas as pl
from jax.experimental.pallas import tpu as pltpu
from jax.sharding import PartitionSpec as P

HEAD_DIM = 128
MAX_TILES = 4
KEY_ROWS = 256
TEXT_CHUNKS = 4
TILE = 16
TERMS = 6
MOST_IN_PLACE = 8 << 20
LOWEST = -1e30
SCALE = 1.0 / math.sqrt(HEAD_DIM)
SCALE_LOG2 = SCALE / math.log(2.0)
BF16 = jnp.bfloat16
F32 = jnp.float32

SMEM = pl.BlockSpec(memory_space=pltpu.SMEM)
VMEM = pl.BlockSpec(memory_space=pltpu.VMEM)
ANY = pl.BlockSpec(memory_space=pl.ANY)
HBM = pl.BlockSpec(memory_space=pltpu.HBM)


def whole_tiles(rows):
    return -(-rows // TILE) * TILE


def exchange(block, axis, distance):
    count = lax.axis_size(axis)
    return lax.ppermute(block, axis, [(i, i ^ distance) for i in range(count)])


def call(kernel, out_shape, in_specs, scratch, args, out_specs=None, grid=(), megabytes=16, cost=0):
    many = isinstance(out_shape, (list, tuple))
    if out_specs is None:
        out_specs = [VMEM] * len(out_shape) if many else VMEM
    return pl.pallas_call(
        kernel,
        out_shape=out_shape,
        in_specs=in_specs,
        out_specs=out_specs,
        grid=grid,
        name=getattr(kernel, "func", kernel).__name__,
        scratch_shapes=scratch,
        compiler_params=pltpu.CompilerParams(vmem_limit_bytes=megabytes << 20),
        cost_estimate=pl.CostEstimate(flops=cost * 10**9, bytes_accessed=0, transcendentals=0),
    )(*args)


def place_of(perm_ref, owner, owners):
    first = jnp.int32(0)
    for index in range(owners):
        first = first + jnp.where(perm_ref[index] == owner, index, 0)
    return first


def sample_at(count_ref, place, samples):
    end, sample, start = jnp.int32(0), jnp.int32(0), jnp.int32(0)
    for index in range(samples):
        end = end + count_ref[index]
        passed = place >= end
        sample = sample + passed.astype(jnp.int32)
        start = jnp.where(passed, end, start)
    return sample, start


def pack_kernel(heads, who, length, *refs):
    inputs, outs, buffers, sem = refs[:3], refs[3:-4], refs[-4:-1], refs[-1]
    copies = [pltpu.make_async_copy(a, b, sem.at[i]) for i, (a, b) in enumerate(zip(inputs, buffers))]
    for copy in copies:
        copy.start()
    for copy in copies:
        copy.wait()
    q_ref, o_ref, g_ref = buffers
    rows = q_ref.shape[0]
    seq = who[0]
    position = seq * rows + lax.broadcasted_iota(jnp.int32, (rows, HEAD_DIM), 0)
    keep = position < length[0]
    for j, out in enumerate(outs):
        place = lax.broadcasted_iota(jnp.int32, (out.shape[0] - 2 * heads * rows, HEAD_DIM), 0)
        deltas = jnp.zeros(place.shape, F32)
        for h in range(heads):
            columns = pl.ds(pl.multiple_of(((seq ^ j) * heads + h) * HEAD_DIM, HEAD_DIM), HEAD_DIM)
            grad = jnp.where(keep, g_ref[:, columns].astype(F32), 0.0)
            product = grad * o_ref[:, columns].astype(F32)
            delta = jnp.sum(jnp.transpose(product), axis=0, keepdims=True)
            out[h * rows:(h + 1) * rows] = q_ref[:, columns]
            out[(heads + h) * rows:(heads + h + 1) * rows] = grad.astype(BF16)
            deltas = jnp.where(place == j * heads + h, delta, deltas)
        out[2 * heads * rows:] = deltas.astype(BF16)


def stack_kernel(count, rows, extra, *refs):
    out, buffer, sem = refs[-3:]
    size = rows.stop - rows.start
    copies = [
        pltpu.make_async_copy(refs[i].at[rows], out.at[pl.ds(i * size, size)], sem.at[0, i]) for i in range(count)
    ]
    if extra:
        last = pl.ds(refs[0].shape[0] - extra, extra)
        copies += [pltpu.make_async_copy(refs[i].at[last], buffer.at[i], sem.at[1, i]) for i in range(count)]
    for copy in copies:
        copy.start()
    for copy in copies:
        copy.wait()
    if extra:
        out[count * size:] = sum(buffer[i].astype(F32) for i in range(count)).astype(BF16)


def join_kernel(count, *refs):
    out, sem = refs[-2], refs[-1]
    copies = [pltpu.make_async_copy(refs[i], out.at[i], sem.at[i]) for i in range(count)]
    for copy in copies:
        copy.start()
    for copy in copies:
        copy.wait()


def by_distance(groups, refs):
    found = {}
    for index, group in enumerate(groups):
        for place, chip in enumerate(group):
            for core in range(2):
                found[2 * chip + core] = refs[2 * index + core].at[place]
    return [found[distance] for distance in range(len(found))]


def fetch(pieces, relative, target, sem):
    for distance, piece in enumerate(pieces):
        @pl.when(relative == distance)
        def _(piece=piece):
            pltpu.make_async_copy(piece, target, sem).start()


def spans_of(rows):
    full = rows // KEY_ROWS
    tail = rows - full * KEY_ROWS
    return [(i * KEY_ROWS, KEY_ROWS, KEY_ROWS) for i in range(full)] + [(full * KEY_ROWS, -(-tail // 16) * 16, tail)]


def dot_nt(a, b):
    return lax.dot_general(a, b, (((1,), (1,)), ((), ())), preferred_element_type=F32)


def dot_nn(a, b):
    return jnp.dot(a, b, preferred_element_type=F32)


def own_tiles(owners, slots, who, counts, perm):
    first = place_of(perm, who[1], owners)
    return [sample_at(counts, first + slot * owners, owners) for slot in range(slots)]


def pad_kernel(tiles, *refs):
    out = refs[-1]
    for slot in range(tiles.shape[0]):
        for low, size, used in spans_of(tiles.shape[1]):
            if size != used:
                out[slot, low:] = jnp.zeros((size, HEAD_DIM), BF16)
            out[slot, low:low + used] = tiles[slot, low:low + used]


def tiles_kernel(slots, rows, who, own, partner, keys, values, turned):
    for odd in range(2):
        @pl.when((who[0] & 1) == odd)
        def _(odd=odd):
            keys[...] = (own, partner)[odd][...]
            values[...] = (own, partner)[1 - odd][...]
    for slot in range(slots):
        for low, size, _ in spans_of(rows):
            turned[slot, :, low:low + size] = jnp.transpose(keys[slot, low:low + size].astype(F32)).astype(BF16)


def over_steps(body, steps, in_place):
    if in_place:
        lax.fori_loop(0, steps, lambda step, carry: (body(step, step), carry)[1], 0)
    else:
        body(pl.program_id(0), 0)


def weights_kernel(owners, heads, blocks, slots, rows, in_place, who, counts, perm, keys, *refs):
    pieces = refs[:owners]
    notes, weights, text_buf, scores_buf, stats, sem = refs[owners:]
    spans = spans_of(rows)
    groups = text_buf.shape[1] // (heads * HEAD_DIM)
    chunks = groups // blocks
    width = chunks * HEAD_DIM
    tiles = own_tiles(owners, slots, who, counts, perm)

    def body(step, index):
        @pl.when(step == 0)
        def _():
            for slot in range(slots):
                @pl.when(tiles[slot][0] < owners)
                def _(slot=slot):
                    fetch(pieces, tiles[slot][0] ^ who[1], text_buf.at[slot], sem.at[slot])

        for slot in range(slots):
            base = slot * heads * blocks

            @pl.when((step == base) & (tiles[slot][0] < owners))
            def _(slot=slot):
                pltpu.make_async_copy(pieces[0], text_buf.at[slot], sem.at[slot]).wait()

            @pl.when((step >= base) & (step < base + heads * blocks) & (tiles[slot][0] < owners))
            def _(slot=slot, base=base):
                head, block = (step - base) // blocks, (step - base) % blocks
                query = rows_of(text_buf.at[slot], heads, head, block, chunks)
                peak = jnp.full((8, width), -jnp.inf, F32)
                for low, size, used in spans:
                    scores = dot_nt(keys[slot, low:low + size], query)
                    if size != used:
                        row = lax.broadcasted_iota(jnp.int32, scores.shape, 0)
                        scores = jnp.where(row < used, scores, -jnp.inf)
                    scores_buf[low:low + size] = scores
                    peak = jnp.maximum(peak, jnp.max(scores.reshape(-1, 8, width), axis=0))
                top = jnp.max(peak, axis=0, keepdims=True) * SCALE_LOG2
                mass = jnp.zeros((8, width), F32)
                for low, size, used in spans:
                    part = jnp.exp2(scores_buf[low:low + size] * SCALE_LOG2 - top)
                    mass = mass + jnp.sum(part.reshape(-1, 8, width), axis=0)
                    weights[index, low:low + size] = part.astype(BF16)
                stats[2 * head, pl.ds(block, 1)] = top
                stats[2 * head + 1, pl.ds(block, 1)] = jnp.sum(mass, axis=0, keepdims=True)

                @pl.when(step == base + heads * blocks - 1)
                def _():
                    for done in range(blocks):
                        lines = [stats[line, done:done + 1] for line in range(2 * heads)]
                        full = note_rows(lines)
                        size = full.shape[0]
                        for chunk in range(chunks):
                            first = (slot * groups + done * chunks + chunk) * size
                            notes[first:first + size] = full[:, chunk * HEAD_DIM:(chunk + 1) * HEAD_DIM]

    over_steps(body, slots * heads * blocks, in_place)


def in_parts(value):
    high = value.astype(BF16).astype(F32)
    middle = (value - high).astype(BF16).astype(F32)
    return [high, middle, value - high - middle]


def note_rows(lines):
    rows = [term for line in lines for term in in_parts(line)]
    index = lax.broadcasted_iota(jnp.int32, (whole_tiles(len(rows)), lines[0].shape[1]), 0)
    result = jnp.zeros(index.shape, F32)
    for place, row in enumerate(rows):
        result = jnp.where(index == place, row, result)
    return result.astype(BF16)


def read_notes(notes, head):
    notes = notes.astype(F32)
    rows = [notes[place:place + 1] for place in range(TERMS * head, TERMS * head + TERMS)]
    return rows[0] + rows[1] + rows[2], rows[3] + rows[4] + rows[5]


def rows_of(text, heads, head, block, chunks):
    first = block * chunks * heads + head
    starts = [pl.multiple_of((first + chunk * heads) * HEAD_DIM, HEAD_DIM) for chunk in range(chunks)]
    return jnp.concatenate([text[pl.ds(start, HEAD_DIM)] for start in starts], axis=0)


def slopes_kernel(chip_groups, owners, heads, blocks, slots, rows, in_place, who, counts, perm, notes, weights, values, keys_turned, *refs):
    pieces = by_distance(chip_groups, refs[:2 * len(chip_groups)])
    slopes, turned, text_buf, deltas, sem = refs[-5:]
    spans = spans_of(rows)
    groups = turned.shape[2] // HEAD_DIM
    chunks = groups // blocks
    text_rows = groups * heads * HEAD_DIM
    width = chunks * HEAD_DIM
    tiles = own_tiles(owners, slots, who, counts, perm)

    def body(step, index):
        @pl.when(step == 0)
        def _():
            for slot in range(slots):
                @pl.when(tiles[slot][0] < owners)
                def _(slot=slot):
                    fetch(pieces, tiles[slot][0] ^ who[1], text_buf.at[slot], sem.at[slot])

                @pl.when(tiles[slot][0] >= owners)
                def _(slot=slot):
                    turned[slot] = jnp.zeros(turned.shape[1:], BF16)

        for slot in range(slots):
            base = slot * heads * blocks

            @pl.when((step == base) & (tiles[slot][0] < owners))
            def _(slot=slot):
                pltpu.make_async_copy(pieces[0], text_buf.at[slot], sem.at[slot]).wait()
                deltas[...] = text_buf[slot, text_rows:].astype(F32)
                size = turned.shape[1] - heads * HEAD_DIM
                for chunk in range(groups):
                    first = (slot * groups + chunk) * size
                    columns = slice(chunk * HEAD_DIM, (chunk + 1) * HEAD_DIM)
                    turned[slot, heads * HEAD_DIM:, columns] = notes[first:first + size]

            @pl.when((step >= base) & (step < base + heads * blocks) & (tiles[slot][0] < owners))
            def _(slot=slot, base=base):
                head, block = (step - base) // blocks, (step - base) % blocks
                grad = rows_of(text_buf.at[slot], heads, head, block, chunks)
                first = block * chunks * heads + head
                delta = jnp.concatenate([deltas[pl.ds(first + chunk * heads, 1)] for chunk in range(chunks)], axis=1)
                for low, size, used in spans:
                    slope = dot_nt(values[slot, low:low + size], grad)
                    slopes[index, low:low + size] = (weights[index, low:low + size].astype(F32) * (slope - delta)).astype(BF16)
                total = dot_nn(keys_turned[slot, :, :slopes.shape[1]], slopes[index])
                columns = pl.ds(pl.multiple_of(block * width, width), width)
                turned[slot, pl.ds(pl.multiple_of(head * HEAD_DIM, HEAD_DIM), HEAD_DIM), columns] = total.astype(BF16)

    over_steps(body, slots * heads * blocks, in_place)


def peak_and_mass(notes, owners, heads, groups, me, perm, start, tiles, head, chunk):
    found = []
    size = whole_tiles(TERMS * heads)
    for index in range(MAX_TILES):
        live = index < tiles
        place = jnp.where(live, start + index, start)
        other, slot = perm[place & (owners - 1)] ^ me, lax.div(place, owners)
        first = pl.multiple_of((slot * groups + chunk) * size, size)
        top, mass = read_notes(notes[other, pl.ds(first, size)], head)
        found.append((jnp.where(live, top, -jnp.inf), jnp.where(live, mass, 0.0)))
    top = functools.reduce(jnp.maximum, [peak for peak, _ in found])
    return top, sum(mass * jnp.exp2(peak - top) for peak, mass in found)


def factors_kernel(owners, heads, groups, slots, who, counts, perm, own, other, out, notes):
    for chip in range(owners // 2):
        notes[2 * chip] = own[chip]
        notes[2 * chip + 1] = other[chip]
    size = whole_tiles(TERMS * heads)
    for slot, (sample, start) in enumerate(own_tiles(owners, slots, who, counts, perm)):
        @pl.when(sample < owners)
        def _(slot=slot, sample=sample, start=start):
            tiles = counts[jnp.minimum(sample, owners - 1)]
            for head in range(heads):
                for chunk in range(groups):
                    top, mass = peak_and_mass(
                        notes, owners, heads, groups, who[1], perm, start, tiles, head, chunk
                    )
                    first = (slot * groups + chunk) * size
                    peak = read_notes(notes[0, first:first + size], head)[0]
                    out[slot, head, chunk:chunk + 1] = jnp.exp2(peak - top) / mass


def sums_kernel(owners, heads, blocks, slots, slot, in_place, who, counts, perm, *refs):
    weights, slopes, factors, q_buf, g_buf = refs[:5]
    keep_out, send_out, sums = refs[-3:]
    odd = who[0] & 1
    groups = q_buf.shape[1] // (heads * HEAD_DIM)
    chunks = groups // blocks
    width = chunks * HEAD_DIM
    sample = own_tiles(owners, slots, who, counts, perm)[slot][0]
    used = sample < owners

    def body(step, index):
        @pl.when(jnp.logical_not(used))
        def _():
            keep_out[...] = jnp.zeros(keep_out.shape, BF16)
            send_out[...] = jnp.zeros(send_out.shape, BF16)

        @pl.when(used)
        def _():
            head, block = step // blocks, step % blocks
            factor = jnp.concatenate(
                [factors[slot, head, pl.ds(block * chunks + chunk, 1)] for chunk in range(chunks)], axis=1
            )
            factor = jnp.transpose(jnp.broadcast_to(factor, (HEAD_DIM, width)))
            query = rows_of(q_buf.at[slot], heads, head, block, chunks)
            grad = rows_of(g_buf.at[slot], heads, head, block, chunks)
            query = (query.astype(F32) * factor * SCALE).astype(BF16)
            grad = (grad.astype(F32) * factor).astype(BF16)

            def add(which, source, right, fresh):
                for low in range(0, sums.shape[1], 2 * KEY_ROWS):
                    span = slice(low, min(low + 2 * KEY_ROWS, sums.shape[1]))
                    part = dot_nn(source[index, span], right)
                    sums[which, span] = part if fresh else sums[which, span] + part

            for fresh in (True, False):
                @pl.when((step == 0) == fresh)
                def _(fresh=fresh):
                    add(0, slopes, query, fresh)
                    add(1, weights, grad, fresh)

            @pl.when(step == heads * blocks - 1)
            def _():
                keep_out[...] = sums[odd].astype(BF16)
                send_out[...] = sums[1 - odd].astype(BF16)

    steps = heads * blocks
    over_steps(lambda step, index: body(step, slot * steps + index if in_place else index), steps, in_place)


def route_kernel(owners, heads, blocks, slots, who, counts, perm, own, other, *refs):
    outs = refs[-(owners // 2):]
    me = who[1]
    width = own.shape[2] // blocks
    split = heads * HEAD_DIM
    found = []
    for near in range(2):
        first = place_of(perm, me ^ near, owners)
        for slot in range(slots):
            found.append((near, slot, sample_at(counts, first + slot * owners, owners)[0]))

    def one(block, carry):
        columns = pl.ds(pl.multiple_of(block * width, width), width)
        sources = [(own, other)[near].at[slot] for near, slot, _ in found]
        notes = [source[split:, columns] for source in sources]
        lines = [[] for _ in outs]
        for head in range(heads):
            rows = slice(head * HEAD_DIM, (head + 1) * HEAD_DIM)
            parts = [source[rows, columns].astype(F32) for source in sources]
            known = [read_notes(note, head) for note in notes]
            for distance, out in enumerate(outs):
                live = [sample == me ^ (2 * distance) for _, _, sample in found]
                tops = [jnp.where(hit, note[0], LOWEST) for hit, note in zip(live, known)]
                top = functools.reduce(jnp.maximum, tops)
                factors = [jnp.where(hit, jnp.exp2(peak - top), 0.0) for hit, peak in zip(live, tops)]
                mass = sum(note[1] * factor for note, factor in zip(known, factors))
                out[rows, columns] = sum(part * factor for part, factor in zip(parts, factors)).astype(BF16)
                lines[distance] += [top, mass]
        for distance, out in enumerate(outs):
            out[split:, columns] = note_rows(lines[distance])
        return carry

    lax.fori_loop(0, blocks, one, 0)


def gather_kernel(heads, parts, *refs):
    outs = refs[parts:]
    rows = outs[0].shape[0]
    split = heads * HEAD_DIM
    for piece, out in enumerate(outs):
        span = slice(piece * rows, (piece + 1) * rows)
        blocks = [ref[split:, span] for ref in refs[:parts]]
        for head in range(heads):
            lanes = slice(head * HEAD_DIM, (head + 1) * HEAD_DIM)
            notes = [read_notes(block, head) for block in blocks]
            top = functools.reduce(jnp.maximum, [note[0] for note in notes])
            factors = [jnp.exp2(note[0] - top) for note in notes]
            mass = sum(note[1] * factor for note, factor in zip(notes, factors))
            total = sum(ref[lanes, span].astype(F32) * factor for ref, factor in zip(refs[:parts], factors))
            out[:, lanes] = jnp.transpose(total * (SCALE / mass)).astype(BF16)


def place_kernel(who, *refs):
    out = refs[-1]
    for distance, ref in enumerate(refs[:-2]):
        width = ref.shape[1]
        start = pl.multiple_of((who[0] ^ distance) * width, width)
        out[:, pl.ds(start, width)] = ref[...]


def merge_kernel(slots, *refs):
    keep, got, out, done = refs[:slots], refs[slots:-2], refs[-2], refs[-1]
    done[...] = jnp.zeros(done.shape, BF16)
    for low, size, used in spans_of(out.shape[0]):
        row = lax.broadcasted_iota(jnp.int32, (slots * size, slots * size), 0)
        column = lax.broadcasted_iota(jnp.int32, (slots * size, slots * size), 1)
        source = lax.rem(row, slots) * size + lax.div(row, slots)
        order = (source == column).astype(BF16)
        total = [
            (keep[slot][low:low + size].astype(F32) + got[slot][low:low + size].astype(F32)).astype(BF16)
            for slot in range(slots)
        ]
        mixed = dot_nn(order, jnp.concatenate(total, axis=0)).astype(BF16).reshape(size, slots, HEAD_DIM)
        out[low:low + used] = mixed[:used]


def shards(queries, saved_output, grad_out, tile_kv, tile_count, owner_perm, text_len):
    rows_dev, features = queries.shape[1], queries.shape[2]
    groups, owners = lax.axis_size("seq"), lax.axis_size("dp")
    heads = features // HEAD_DIM // groups
    width = heads * HEAD_DIM
    chunks = min(TEXT_CHUNKS, groups)
    blocks = groups // chunks
    text_rows, block_rows = groups * rows_dev, chunks * rows_dev
    steps = heads * blocks
    slots, tile_rows = tile_kv.shape[0], tile_kv.shape[1]
    low, tail_rows, _ = spans_of(tile_rows)[-1]
    padded = low + tail_rows
    who = jnp.stack([lax.axis_index("seq"), lax.axis_index("dp")]).astype(jnp.int32)
    known = (who, tile_count, owner_perm)
    scale = blocks

    delta_rows = whole_tiles(groups * heads)
    piece_rows = 2 * heads * rows_dev + delta_rows
    note_size = whole_tiles(TERMS * heads)
    note_count = slots * groups * note_size
    packed = call(
        functools.partial(pack_kernel, heads),
        [jax.ShapeDtypeStruct((piece_rows, HEAD_DIM), BF16)] * groups,
        [SMEM, SMEM] + [HBM] * 3,
        [pltpu.VMEM((rows_dev, features), BF16)] * 3 + [pltpu.SemaphoreType.DMA((3,))],
        (who, text_len, queries[0], saved_output[0], grad_out[0]),
        megabytes=16,
        cost=1,
    )
    pieces = [packed[0]] + [exchange(packed[j], "seq", j) for j in range(1, groups)]
    tile_shape = jax.ShapeDtypeStruct((slots, padded, HEAD_DIM), BF16)
    own_tile = call(pad_kernel, tile_shape, [VMEM] + [ANY] * (groups - 1), [], (tile_kv, *pieces[1:]), cost=1)
    partner_tile = exchange(own_tile, "seq", 1)

    def near_of(first, extra, order):
        block = call(
            functools.partial(stack_kernel, groups, slice(first, first + heads * rows_dev), extra),
            jax.ShapeDtypeStruct((groups * heads * rows_dev + extra, HEAD_DIM), BF16),
            [HBM] + [ANY] * (groups - 1 + len(order)),
            [pltpu.VMEM((groups, delta_rows, HEAD_DIM), BF16), pltpu.SemaphoreType.DMA((2, groups))],
            (*pieces, *order),
            megabytes=8 * scale,
        )
        return near(block)

    def near(block):
        return [block] + [exchange(block, "dp", d) for d in range(2, owners, 2)]

    q_near = near_of(0, 0, [own_tile])
    g_near = near_of(heads * rows_dev, delta_rows, q_near[1:2])
    q_all = [block for piece in q_near for block in (piece, exchange(piece, "dp", 1))]

    turn_shape = jax.ShapeDtypeStruct((slots, HEAD_DIM, -(-padded // HEAD_DIM) * HEAD_DIM), BF16)
    keys, values, keys_turned = call(
        functools.partial(tiles_kernel, slots, tile_rows),
        [tile_shape, tile_shape, turn_shape],
        [SMEM] + [VMEM] * 2,
        [],
        (who, own_tile, partner_tile),
        cost=0,
    )
    stack_shape = jax.ShapeDtypeStruct((slots * steps, padded, block_rows), BF16)
    in_place = 2 * math.prod(stack_shape.shape) <= MOST_IN_PLACE
    stack_spec = VMEM if in_place else pl.BlockSpec((1, padded, block_rows), lambda i: (i, 0, 0))
    notes, weights, q_own = call(
        functools.partial(weights_kernel, owners, heads, blocks, slots, tile_rows, in_place),
        [
            jax.ShapeDtypeStruct((note_count, HEAD_DIM), BF16),
            stack_shape,
            jax.ShapeDtypeStruct((slots,) + q_near[0].shape, BF16),
        ],
        [SMEM] * 3 + [VMEM] + [ANY] * owners,
        [
            pltpu.VMEM((padded, block_rows), F32),
            pltpu.VMEM((2 * heads, blocks, block_rows), F32),
            pltpu.SemaphoreType.DMA((slots,)),
        ],
        (*known, keys, *q_all),
        out_specs=[VMEM, stack_spec, VMEM],
        grid=() if in_place else (slots * steps,),
        megabytes=16,
        cost=0,
    )
    def over_core(blocks_near, order):
        joined = call(
            functools.partial(join_kernel, len(blocks_near)),
            jax.ShapeDtypeStruct((len(blocks_near),) + blocks_near[0].shape, BF16),
            [ANY] * (len(blocks_near) + len(order)),
            [pltpu.SemaphoreType.DMA((len(blocks_near),))],
            (*blocks_near, *order),
            megabytes=12 * scale,
        )
        return [joined, exchange(joined, "dp", 1)]

    notes_near = near(notes)
    direct = [chip for chip in range(1, owners // 2) if chip & (chip - 1) == 0]
    chip_groups = [[chip for chip in range(owners // 2) if chip not in direct], direct]
    g_pairs = []
    for group in chip_groups:
        g_pairs += over_core([g_near[chip] for chip in group], [notes])
    slopes, part, g_own = call(
        functools.partial(slopes_kernel, chip_groups, owners, heads, blocks, slots, tile_rows, in_place),
        [
            stack_shape,
            jax.ShapeDtypeStruct((slots, width + note_size, text_rows), BF16),
            jax.ShapeDtypeStruct((slots,) + g_near[0].shape, BF16),
        ],
        [SMEM] * 3 + [VMEM, stack_spec] + [VMEM] * 2 + [ANY] * len(g_pairs),
        [
            pltpu.VMEM((delta_rows, HEAD_DIM), F32),
            pltpu.SemaphoreType.DMA((slots,)),
        ],
        (*known, notes, weights, values, keys_turned, *g_pairs),
        out_specs=[stack_spec, VMEM, VMEM],
        grid=() if in_place else (slots * steps,),
        megabytes=20,
        cost=6,
    )
    notes_pair = over_core(notes_near, [part])
    factors = call(
        functools.partial(factors_kernel, owners, heads, groups, slots),
        jax.ShapeDtypeStruct((slots, heads, groups, HEAD_DIM), F32),
        [SMEM] * 3 + [VMEM] * 2,
        [pltpu.VMEM((owners, note_count, HEAD_DIM), BF16)],
        (*known, *notes_pair),
        cost=30,
    )
    kept, got = [], []

    def tile_sums(slot, order):
        left_spec = VMEM if in_place else pl.BlockSpec((1, padded, block_rows), lambda i: (slot * steps + i, 0, 0))
        keep, send = call(
            functools.partial(sums_kernel, owners, heads, blocks, slots, slot, in_place),
            [jax.ShapeDtypeStruct((padded, HEAD_DIM), BF16)] * 2,
            [SMEM] * 3 + [left_spec] * 2 + [VMEM] * 3 + [ANY] * len(order),
            [pltpu.VMEM((2, padded, HEAD_DIM), F32)],
            (*known, weights, slopes, factors, q_own, g_own, *order),
            out_specs=[VMEM] * 2,
            grid=() if in_place else (steps,),
            megabytes=8 * scale,
            cost=4,
        )
        kept.append(keep)
        got.append(exchange(send, "seq", 1))

    tile_sums(0, [])
    routed = call(
        functools.partial(route_kernel, owners, heads, blocks, slots),
        [jax.ShapeDtypeStruct((width + note_size, text_rows), BF16)] * (owners // 2),
        [SMEM] * 3 + [VMEM] * 2 + [ANY] * 2,
        [],
        (*known, part, exchange(part, "dp", 1), factors, kept[0]),
        megabytes=14,
        cost=30,
    )

    for slot in range(1, slots):
        tile_sums(slot, [routed[0]])

    sums = [routed[0]] + [exchange(routed[d], "dp", 2 * d) for d in range(1, owners // 2)]
    cut = call(
        functools.partial(gather_kernel, heads, len(sums)),
        [jax.ShapeDtypeStruct((rows_dev, width), BF16)] * groups,
        [VMEM] * len(sums),
        [],
        sums,
        megabytes=8 * scale,
        cost=30,
    )
    back = [cut[0]] + [exchange(cut[j], "seq", j) for j in range(1, groups)]
    grad_tiles, merged = call(
        functools.partial(merge_kernel, slots),
        [jax.ShapeDtypeStruct((tile_rows, slots, HEAD_DIM), BF16), jax.ShapeDtypeStruct((TILE, HEAD_DIM), BF16)],
        [VMEM] * (2 * slots),
        [],
        (*kept, *got),
        cost=2,
    )
    grad_queries = call(
        place_kernel,
        jax.ShapeDtypeStruct((rows_dev, features), BF16),
        [SMEM] + [VMEM] * groups + [ANY],
        [],
        (who, *back, merged),
        cost=1,
    )
    return (grad_queries[None], jnp.transpose(grad_tiles, (1, 0, 2)))


def solution(mesh):
    placed = (
        P("dp", "seq", None),
        P("dp", "seq", None),
        P("dp", "seq", None),
        P("dp", None, "seq"),
        P(),
        P(),
        P("dp"),
    )
    return jax.shard_map(
        shards,
        mesh=mesh,
        in_specs=placed,
        out_specs=(P("dp", "seq", None), P("dp", None, "seq")),
        check_vma=False,
    )
```

```python
import functools
import math

import jax
import jax.numpy as jnp
from jax import lax
from jax.experimental import pallas as pl
from jax.experimental.pallas import tpu as pltpu
from jax.sharding import PartitionSpec as P

HEAD_DIM = 128
MAX_TILES = 4
KEY_ROWS = 256
TEXT_CHUNKS = 4
TILE = 16
TERMS = 6
MOST_IN_PLACE = 8 << 20
LOWEST = -1e30
SCALE = 1.0 / math.sqrt(HEAD_DIM)
SCALE_LOG2 = SCALE / math.log(2.0)
BF16 = jnp.bfloat16
F32 = jnp.float32

SMEM = pl.BlockSpec(memory_space=pltpu.SMEM)
VMEM = pl.BlockSpec(memory_space=pltpu.VMEM)
ANY = pl.BlockSpec(memory_space=pl.ANY)
HBM = pl.BlockSpec(memory_space=pltpu.HBM)


def whole_tiles(rows):
    return -(-rows // TILE) * TILE


def exchange(block, axis, distance):
    count = lax.axis_size(axis)
    return lax.ppermute(block, axis, [(i, i ^ distance) for i in range(count)])


def call(kernel, out_shape, in_specs, scratch, args, out_specs=None, grid=(), megabytes=16, cost=0):
    many = isinstance(out_shape, (list, tuple))
    if out_specs is None:
        out_specs = [VMEM] * len(out_shape) if many else VMEM
    return pl.pallas_call(
        kernel,
        out_shape=out_shape,
        in_specs=in_specs,
        out_specs=out_specs,
        grid=grid,
        name=getattr(kernel, "func", kernel).__name__,
        scratch_shapes=scratch,
        compiler_params=pltpu.CompilerParams(vmem_limit_bytes=megabytes << 20),
        cost_estimate=pl.CostEstimate(flops=cost * 10**9, bytes_accessed=0, transcendentals=0),
    )(*args)


def place_of(perm_ref, owner, owners):
    first = jnp.int32(0)
    for index in range(owners):
        first = first + jnp.where(perm_ref[index] == owner, index, 0)
    return first


def sample_at(count_ref, place, samples):
    end, sample, start = jnp.int32(0), jnp.int32(0), jnp.int32(0)
    for index in range(samples):
        end = end + count_ref[index]
        passed = place >= end
        sample = sample + passed.astype(jnp.int32)
        start = jnp.where(passed, end, start)
    return sample, start


def pack_kernel(heads, who, length, *refs):
    inputs, outs, buffers, sem = refs[:3], refs[3:-4], refs[-4:-1], refs[-1]
    copies = [pltpu.make_async_copy(a, b, sem.at[i]) for i, (a, b) in enumerate(zip(inputs, buffers))]
    for copy in copies:
        copy.start()
    for copy in copies:
        copy.wait()
    q_ref, o_ref, g_ref = buffers
    rows = q_ref.shape[0]
    seq = who[0]
    position = seq * rows + lax.broadcasted_iota(jnp.int32, (rows, HEAD_DIM), 0)
    keep = position < length[0]
    for j, out in enumerate(outs):
        place = lax.broadcasted_iota(jnp.int32, (out.shape[0] - 2 * heads * rows, HEAD_DIM), 0)
        deltas = jnp.zeros(place.shape, F32)
        for h in range(heads):
            columns = pl.ds(pl.multiple_of(((seq ^ j) * heads + h) * HEAD_DIM, HEAD_DIM), HEAD_DIM)
            grad = jnp.where(keep, g_ref[:, columns].astype(F32), 0.0)
            product = grad * o_ref[:, columns].astype(F32)
            delta = jnp.sum(jnp.transpose(product), axis=0, keepdims=True)
            out[h * rows:(h + 1) * rows] = q_ref[:, columns]
            out[(heads + h) * rows:(heads + h + 1) * rows] = grad.astype(BF16)
            deltas = jnp.where(place == j * heads + h, delta, deltas)
        out[2 * heads * rows:] = deltas.astype(BF16)


def stack_kernel(count, rows, extra, *refs):
    out, buffer, sem = refs[-3:]
    size = rows.stop - rows.start
    copies = [
        pltpu.make_async_copy(refs[i].at[rows], out.at[pl.ds(i * size, size)], sem.at[0, i]) for i in range(count)
    ]
    if extra:
        last = pl.ds(refs[0].shape[0] - extra, extra)
        copies += [pltpu.make_async_copy(refs[i].at[last], buffer.at[i], sem.at[1, i]) for i in range(count)]
    for copy in copies:
        copy.start()
    for copy in copies:
        copy.wait()
    if extra:
        out[count * size:] = sum(buffer[i].astype(F32) for i in range(count)).astype(BF16)


def join_kernel(count, *refs):
    out, sem = refs[-2], refs[-1]
    copies = [pltpu.make_async_copy(refs[i], out.at[i], sem.at[i]) for i in range(count)]
    for copy in copies:
        copy.start()
    for copy in copies:
        copy.wait()


def by_distance(groups, refs):
    found = {}
    for index, group in enumerate(groups):
        for place, chip in enumerate(group):
            for core in range(2):
                found[2 * chip + core] = refs[2 * index + core].at[place]
    return [found[distance] for distance in range(len(found))]


def fetch(pieces, relative, targets, sems):
    for distance, blocks in enumerate(pieces):
        @pl.when(relative == distance)
        def _(blocks=blocks):
            for block, target, sem in zip(blocks, targets, sems):
                pltpu.make_async_copy(block, target, sem).start()


def await_fetch(pieces, targets, sems):
    for block, target, sem in zip(pieces[0], targets, sems):
        pltpu.make_async_copy(block, target, sem).wait()


def spans_of(rows):
    full = rows // KEY_ROWS
    tail = rows - full * KEY_ROWS
    return [(i * KEY_ROWS, KEY_ROWS, KEY_ROWS) for i in range(full)] + [(full * KEY_ROWS, -(-tail // 16) * 16, tail)]


def dot_nt(a, b):
    return lax.dot_general(a, b, (((1,), (1,)), ((), ())), preferred_element_type=F32)


def dot_nn(a, b):
    return jnp.dot(a, b, preferred_element_type=F32)


def own_tiles(owners, slots, who, counts, perm):
    first = place_of(perm, who[1], owners)
    return [sample_at(counts, first + slot * owners, owners) for slot in range(slots)]


def pad_kernel(tiles, *refs):
    out = refs[-1]
    for slot in range(tiles.shape[0]):
        for low, size, used in spans_of(tiles.shape[1]):
            if size != used:
                out[slot, low:] = jnp.zeros((size, HEAD_DIM), BF16)
            out[slot, low:low + used] = tiles[slot, low:low + used]


def tiles_kernel(slots, rows, who, own, partner, keys, values, turned):
    for odd in range(2):
        @pl.when((who[0] & 1) == odd)
        def _(odd=odd):
            keys[...] = (own, partner)[odd][...]
            values[...] = (own, partner)[1 - odd][...]
    for slot in range(slots):
        for low, size, _ in spans_of(rows):
            turned[slot, :, low:low + size] = jnp.transpose(keys[slot, low:low + size].astype(F32)).astype(BF16)


def over_steps(body, steps, in_place):
    if in_place:
        lax.fori_loop(0, steps, lambda step, carry: (body(step, step), carry)[1], 0)
    else:
        body(pl.program_id(0), 0)


def weights_kernel(owners, heads, blocks, slots, rows, in_place, who, counts, perm, keys, *refs):
    pieces = [[piece] for piece in refs[:owners]]
    notes, weights, text_buf, scores_buf, stats, sem = refs[owners:]
    spans = spans_of(rows)
    groups = text_buf.shape[1] // (heads * HEAD_DIM)
    chunks = groups // blocks
    width = chunks * HEAD_DIM
    tiles = own_tiles(owners, slots, who, counts, perm)

    def score(slot, query, buffer, span, peak):
        low, size, used = span
        scores = dot_nt(keys[slot, low:low + size], query)
        if size != used:
            row = lax.broadcasted_iota(jnp.int32, scores.shape, 0)
            scores = jnp.where(row < used, scores, -jnp.inf)
        scores_buf[buffer, low:low + size] = scores
        return jnp.maximum(peak, jnp.max(scores.reshape(-1, 8, width), axis=0))

    def weigh(index, buffer, span, top, mass):
        low, size, _ = span
        part = jnp.exp2(scores_buf[buffer, low:low + size] * SCALE_LOG2 - top)
        weights[index, low:low + size] = part.astype(BF16)
        return mass + jnp.sum(part.reshape(-1, 8, width), axis=0)

    lowest = jnp.full((8, width), -jnp.inf, F32)
    nothing = jnp.zeros((8, width), F32)

    def tile_weights(slot, items):
        before = None
        for buffer, item in enumerate(items + [None]):
            peak, mass = lowest, nothing
            if item is not None:
                query = rows_of(text_buf.at[slot], heads, item[1], item[2], chunks)
            for span in spans:
                if item is not None:
                    peak = score(slot, query, buffer % 2, span, peak)
                if before is not None:
                    mass = weigh(before[0][0], (buffer + 1) % 2, span, before[1], mass)
            if before is not None:
                (_, head, block), top = before
                stats[2 * head, pl.ds(block, 1)] = top
                stats[2 * head + 1, pl.ds(block, 1)] = jnp.sum(mass, axis=0, keepdims=True)
            before = (item, jnp.max(peak, axis=0, keepdims=True) * SCALE_LOG2)

    def write_notes(slot):
        for done in range(blocks):
            lines = [stats[line, done:done + 1] for line in range(2 * heads)]
            full = note_rows(lines)
            size = full.shape[0]
            for chunk in range(chunks):
                begin = (slot * groups + done * chunks + chunk) * size
                notes[begin:begin + size] = full[:, chunk * HEAD_DIM:(chunk + 1) * HEAD_DIM]

    def start_fetches():
        for slot in range(slots):
            @pl.when(tiles[slot][0] < owners)
            def _(slot=slot):
                fetch(pieces, tiles[slot][0] ^ who[1], [text_buf.at[slot]], [sem.at[slot]])

    def wait_fetch(slot):
        await_fetch(pieces, [text_buf.at[slot]], [sem.at[slot]])

    steps = heads * blocks
    if in_place:
        start_fetches()
        for slot in range(slots):
            @pl.when(tiles[slot][0] < owners)
            def _(slot=slot):
                wait_fetch(slot)
                tile_weights(slot, [(slot * steps + i, i // blocks, i % blocks) for i in range(steps)])
                write_notes(slot)
        return

    step = pl.program_id(0)
    pl.when(step == 0)(start_fetches)
    for slot in range(slots):
        base = slot * steps

        @pl.when((step >= base) & (step < base + steps) & (tiles[slot][0] < owners))
        def _(slot=slot, base=base):
            pl.when(step == base)(lambda: wait_fetch(slot))
            tile_weights(slot, [(0, (step - base) // blocks, (step - base) % blocks)])
            pl.when(step == base + steps - 1)(lambda: write_notes(slot))


def in_parts(value):
    high = value.astype(BF16).astype(F32)
    middle = (value - high).astype(BF16).astype(F32)
    return [high, middle, value - high - middle]


def note_rows(lines):
    rows = [term for line in lines for term in in_parts(line)]
    index = lax.broadcasted_iota(jnp.int32, (whole_tiles(len(rows)), lines[0].shape[1]), 0)
    result = jnp.zeros(index.shape, F32)
    for place, row in enumerate(rows):
        result = jnp.where(index == place, row, result)
    return result.astype(BF16)


def read_notes(notes, head):
    notes = notes.astype(F32)
    rows = [notes[place:place + 1] for place in range(TERMS * head, TERMS * head + TERMS)]
    return rows[0] + rows[1] + rows[2], rows[3] + rows[4] + rows[5]


def rows_of(text, heads, head, block, chunks):
    first = block * chunks * heads + head
    starts = [pl.multiple_of((first + chunk * heads) * HEAD_DIM, HEAD_DIM) for chunk in range(chunks)]
    return jnp.concatenate([text[pl.ds(start, HEAD_DIM)] for start in starts], axis=0)


def slopes_kernel(chip_groups, owners, heads, blocks, slots, rows, in_place, who, counts, perm, notes, weights, values, keys_turned, *refs):
    pieces = [[piece] for piece in by_distance(chip_groups, refs[:2 * len(chip_groups)])]
    slopes, turned, text_buf, deltas, sem = refs[-5:]
    spans = spans_of(rows)
    groups = turned.shape[2] // HEAD_DIM
    chunks = groups // blocks
    text_rows = groups * heads * HEAD_DIM
    width = chunks * HEAD_DIM
    tiles = own_tiles(owners, slots, who, counts, perm)

    def body(step, index):
        @pl.when(step == 0)
        def _():
            for slot in range(slots):
                @pl.when(tiles[slot][0] < owners)
                def _(slot=slot):
                    fetch(pieces, tiles[slot][0] ^ who[1], [text_buf.at[slot]], [sem.at[slot]])

                @pl.when(tiles[slot][0] >= owners)
                def _(slot=slot):
                    turned[slot] = jnp.zeros(turned.shape[1:], BF16)

        for slot in range(slots):
            base = slot * heads * blocks

            @pl.when((step == base) & (tiles[slot][0] < owners))
            def _(slot=slot):
                await_fetch(pieces, [text_buf.at[slot]], [sem.at[slot]])
                deltas[...] = text_buf[slot, text_rows:].astype(F32)
                size = turned.shape[1] - heads * HEAD_DIM
                for chunk in range(groups):
                    first = (slot * groups + chunk) * size
                    columns = slice(chunk * HEAD_DIM, (chunk + 1) * HEAD_DIM)
                    turned[slot, heads * HEAD_DIM:, columns] = notes[first:first + size]

            @pl.when((step >= base) & (step < base + heads * blocks) & (tiles[slot][0] < owners))
            def _(slot=slot, base=base):
                head, block = (step - base) // blocks, (step - base) % blocks
                grad = rows_of(text_buf.at[slot], heads, head, block, chunks)
                first = block * chunks * heads + head
                delta = jnp.concatenate([deltas[pl.ds(first + chunk * heads, 1)] for chunk in range(chunks)], axis=1)
                for low, size, used in spans:
                    slope = dot_nt(values[slot, low:low + size], grad)
                    slopes[index, low:low + size] = (weights[index, low:low + size].astype(F32) * (slope - delta)).astype(BF16)
                total = dot_nn(keys_turned[slot, :, :slopes.shape[1]], slopes[index])
                columns = pl.ds(pl.multiple_of(block * width, width), width)
                turned[slot, pl.ds(pl.multiple_of(head * HEAD_DIM, HEAD_DIM), HEAD_DIM), columns] = total.astype(BF16)

    over_steps(body, slots * heads * blocks, in_place)


def peak_and_mass(notes, owners, heads, groups, me, perm, start, tiles, head, chunk):
    found = []
    size = whole_tiles(TERMS * heads)
    for index in range(MAX_TILES):
        live = index < tiles
        place = jnp.where(live, start + index, start)
        other, slot = perm[place & (owners - 1)] ^ me, lax.div(place, owners)
        first = pl.multiple_of((slot * groups + chunk) * size, size)
        top, mass = read_notes(notes[other, pl.ds(first, size)], head)
        found.append((jnp.where(live, top, -jnp.inf), jnp.where(live, mass, 0.0)))
    top = functools.reduce(jnp.maximum, [peak for peak, _ in found])
    return top, sum(mass * jnp.exp2(peak - top) for peak, mass in found)


def factors_kernel(owners, heads, groups, slots, who, counts, perm, own, other, out, notes):
    for chip in range(owners // 2):
        notes[2 * chip] = own[chip]
        notes[2 * chip + 1] = other[chip]
    size = whole_tiles(TERMS * heads)
    for slot, (sample, start) in enumerate(own_tiles(owners, slots, who, counts, perm)):
        @pl.when(sample < owners)
        def _(slot=slot, sample=sample, start=start):
            tiles = counts[jnp.minimum(sample, owners - 1)]
            for head in range(heads):
                for chunk in range(groups):
                    top, mass = peak_and_mass(
                        notes, owners, heads, groups, who[1], perm, start, tiles, head, chunk
                    )
                    first = (slot * groups + chunk) * size
                    peak = read_notes(notes[0, first:first + size], head)[0]
                    out[slot, head, chunk:chunk + 1] = jnp.exp2(peak - top) / mass


def sums_kernel(owners, heads, blocks, slots, slot, in_place, who, counts, perm, *refs):
    weights, slopes, factors, q_buf, g_buf = refs[:5]
    keep_out, send_out, sums = refs[-3:]
    odd = who[0] & 1
    groups = q_buf.shape[1] // (heads * HEAD_DIM)
    chunks = groups // blocks
    width = chunks * HEAD_DIM
    sample = own_tiles(owners, slots, who, counts, perm)[slot][0]
    used = sample < owners

    def scaled(step):
        head, block = step // blocks, step % blocks
        factor = jnp.concatenate(
            [factors[slot, head, pl.ds(block * chunks + chunk, 1)] for chunk in range(chunks)], axis=1
        )
        factor = jnp.transpose(jnp.broadcast_to(factor, (HEAD_DIM, width)))
        query = rows_of(q_buf.at[slot], heads, head, block, chunks)
        grad = rows_of(g_buf.at[slot], heads, head, block, chunks)
        query = (query.astype(F32) * factor * SCALE).astype(BF16)
        grad = (grad.astype(F32) * factor).astype(BF16)
        return query, grad

    def body(step, index):
        @pl.when(jnp.logical_not(used))
        def _():
            keep_out[...] = jnp.zeros(keep_out.shape, BF16)
            send_out[...] = jnp.zeros(send_out.shape, BF16)

        @pl.when(used)
        def _():
            query, grad = scaled(step)

            def add(which, source, right, fresh):
                for low in range(0, sums.shape[1], 2 * KEY_ROWS):
                    span = slice(low, min(low + 2 * KEY_ROWS, sums.shape[1]))
                    part = dot_nn(source[index, span], right)
                    sums[which, span] = part if fresh else sums[which, span] + part

            for fresh in (True, False):
                @pl.when((step == 0) == fresh)
                def _(fresh=fresh):
                    add(0, slopes, query, fresh)
                    add(1, weights, grad, fresh)

            @pl.when(step == heads * blocks - 1)
            def _():
                keep_out[...] = sums[odd].astype(BF16)
                send_out[...] = sums[1 - odd].astype(BF16)

    steps = heads * blocks
    if not in_place:
        over_steps(body, steps, in_place)
        return

    @pl.when(jnp.logical_not(used))
    def _():
        keep_out[...] = jnp.zeros(keep_out.shape, BF16)
        send_out[...] = jnp.zeros(send_out.shape, BF16)

    @pl.when(used)
    def _():
        rights = [scaled(step) for step in range(steps)]
        for low in range(0, sums.shape[1], KEY_ROWS):
            span = slice(low, min(low + KEY_ROWS, sums.shape[1]))
            for which, source in ((0, slopes), (1, weights)):
                total = sum(dot_nn(source[slot * steps + step, span], rights[step][which]) for step in range(steps))
                sums[which, span] = total.astype(BF16)
        keep_out[...] = sums[odd]
        send_out[...] = sums[1 - odd]


def route_kernel(owners, heads, blocks, slots, who, counts, perm, own, other, *refs):
    outs = refs[-(owners // 2):]
    me = who[1]
    width = own.shape[2] // blocks
    split = heads * HEAD_DIM
    found = []
    for near in range(2):
        first = place_of(perm, me ^ near, owners)
        for slot in range(slots):
            found.append((near, slot, sample_at(counts, first + slot * owners, owners)[0]))

    def one(block, carry):
        columns = pl.ds(pl.multiple_of(block * width, width), width)
        sources = [(own, other)[near].at[slot] for near, slot, _ in found]
        notes = [source[split:, columns] for source in sources]
        lines = [[] for _ in outs]
        for head in range(heads):
            rows = slice(head * HEAD_DIM, (head + 1) * HEAD_DIM)
            parts = [source[rows, columns].astype(F32) for source in sources]
            known = [read_notes(note, head) for note in notes]
            for distance, out in enumerate(outs):
                live = [sample == me ^ (2 * distance) for _, _, sample in found]
                tops = [jnp.where(hit, note[0], LOWEST) for hit, note in zip(live, known)]
                top = functools.reduce(jnp.maximum, tops)
                factors = [jnp.where(hit, jnp.exp2(peak - top), 0.0) for hit, peak in zip(live, tops)]
                mass = sum(note[1] * factor for note, factor in zip(known, factors))
                out[rows, columns] = sum(part * factor for part, factor in zip(parts, factors)).astype(BF16)
                lines[distance] += [top, mass]
        for distance, out in enumerate(outs):
            out[split:, columns] = note_rows(lines[distance])
        return carry

    lax.fori_loop(0, blocks, one, 0)


def gather_kernel(heads, parts, *refs):
    outs = refs[parts:]
    rows = outs[0].shape[0]
    split = heads * HEAD_DIM
    for piece, out in enumerate(outs):
        span = slice(piece * rows, (piece + 1) * rows)
        blocks = [ref[split:, span] for ref in refs[:parts]]
        for head in range(heads):
            lanes = slice(head * HEAD_DIM, (head + 1) * HEAD_DIM)
            notes = [read_notes(block, head) for block in blocks]
            top = functools.reduce(jnp.maximum, [note[0] for note in notes])
            factors = [jnp.exp2(note[0] - top) for note in notes]
            mass = sum(note[1] * factor for note, factor in zip(notes, factors))
            total = sum(ref[lanes, span].astype(F32) * factor for ref, factor in zip(refs[:parts], factors))
            out[:, lanes] = jnp.transpose(total * (SCALE / mass)).astype(BF16)


def place_kernel(who, *refs):
    out = refs[-1]
    for distance, ref in enumerate(refs[:-2]):
        width = ref.shape[1]
        start = pl.multiple_of((who[0] ^ distance) * width, width)
        out[:, pl.ds(start, width)] = ref[...]


def merge_kernel(slots, *refs):
    keep, got, out, done = refs[:slots], refs[slots:-2], refs[-2], refs[-1]
    done[...] = jnp.zeros(done.shape, BF16)
    for low, size, used in spans_of(out.shape[0]):
        row = lax.broadcasted_iota(jnp.int32, (slots * size, slots * size), 0)
        column = lax.broadcasted_iota(jnp.int32, (slots * size, slots * size), 1)
        source = lax.rem(row, slots) * size + lax.div(row, slots)
        order = (source == column).astype(BF16)
        total = [
            (keep[slot][low:low + size].astype(F32) + got[slot][low:low + size].astype(F32)).astype(BF16)
            for slot in range(slots)
        ]
        mixed = dot_nn(order, jnp.concatenate(total, axis=0)).astype(BF16).reshape(size, slots, HEAD_DIM)
        out[low:low + used] = mixed[:used]


def shards(queries, saved_output, grad_out, tile_kv, tile_count, owner_perm, text_len):
    rows_dev, features = queries.shape[1], queries.shape[2]
    groups, owners = lax.axis_size("seq"), lax.axis_size("dp")
    heads = features // HEAD_DIM // groups
    width = heads * HEAD_DIM
    chunks = min(TEXT_CHUNKS, groups)
    blocks = groups // chunks
    text_rows, block_rows = groups * rows_dev, chunks * rows_dev
    steps = heads * blocks
    slots, tile_rows = tile_kv.shape[0], tile_kv.shape[1]
    low, tail_rows, _ = spans_of(tile_rows)[-1]
    padded = low + tail_rows
    who = jnp.stack([lax.axis_index("seq"), lax.axis_index("dp")]).astype(jnp.int32)
    known = (who, tile_count, owner_perm)
    scale = blocks

    delta_rows = whole_tiles(groups * heads)
    piece_rows = 2 * heads * rows_dev + delta_rows
    note_size = whole_tiles(TERMS * heads)
    note_count = slots * groups * note_size
    packed = call(
        functools.partial(pack_kernel, heads),
        [jax.ShapeDtypeStruct((piece_rows, HEAD_DIM), BF16)] * groups,
        [SMEM, SMEM] + [HBM] * 3,
        [pltpu.VMEM((rows_dev, features), BF16)] * 3 + [pltpu.SemaphoreType.DMA((3,))],
        (who, text_len, queries[0], saved_output[0], grad_out[0]),
        megabytes=16,
        cost=1,
    )
    pieces = [packed[0]] + [exchange(packed[j], "seq", j) for j in range(1, groups)]
    tile_shape = jax.ShapeDtypeStruct((slots, padded, HEAD_DIM), BF16)
    own_tile = call(pad_kernel, tile_shape, [VMEM] + [ANY] * (groups - 1), [], (tile_kv, *pieces[1:]), cost=1)
    partner_tile = exchange(own_tile, "seq", 1)

    def near_of(first, extra, order):
        block = call(
            functools.partial(stack_kernel, groups, slice(first, first + heads * rows_dev), extra),
            jax.ShapeDtypeStruct((groups * heads * rows_dev + extra, HEAD_DIM), BF16),
            [HBM] + [ANY] * (groups - 1 + len(order)),
            [pltpu.VMEM((groups, delta_rows, HEAD_DIM), BF16), pltpu.SemaphoreType.DMA((2, groups))],
            (*pieces, *order),
            megabytes=8 * scale,
        )
        return near(block)

    def near(block):
        return [block] + [exchange(block, "dp", d) for d in range(2, owners, 2)]

    q_near = near_of(0, 0, [own_tile])
    g_near = near_of(heads * rows_dev, delta_rows, q_near[1:2])
    q_all = [block for piece in q_near for block in (piece, exchange(piece, "dp", 1))]

    turn_shape = jax.ShapeDtypeStruct((slots, HEAD_DIM, -(-padded // HEAD_DIM) * HEAD_DIM), BF16)
    keys, values, keys_turned = call(
        functools.partial(tiles_kernel, slots, tile_rows),
        [tile_shape, tile_shape, turn_shape],
        [SMEM] + [VMEM] * 2,
        [],
        (who, own_tile, partner_tile),
        cost=0,
    )
    stack_shape = jax.ShapeDtypeStruct((slots * steps, padded, block_rows), BF16)
    in_place = 2 * math.prod(stack_shape.shape) <= MOST_IN_PLACE
    stack_spec = VMEM if in_place else pl.BlockSpec((1, padded, block_rows), lambda i: (i, 0, 0))
    notes, weights, q_own = call(
        functools.partial(weights_kernel, owners, heads, blocks, slots, tile_rows, in_place),
        [
            jax.ShapeDtypeStruct((note_count, HEAD_DIM), BF16),
            stack_shape,
            jax.ShapeDtypeStruct((slots,) + q_near[0].shape, BF16),
        ],
        [SMEM] * 3 + [VMEM] + [ANY] * owners,
        [
            pltpu.VMEM((2, padded, block_rows), F32),
            pltpu.VMEM((2 * heads, blocks, block_rows), F32),
            pltpu.SemaphoreType.DMA((slots,)),
        ],
        (*known, keys, *q_all),
        out_specs=[VMEM, stack_spec, VMEM],
        grid=() if in_place else (slots * steps,),
        megabytes=16,
        cost=0,
    )
    def over_core(blocks_near, order):
        joined = call(
            functools.partial(join_kernel, len(blocks_near)),
            jax.ShapeDtypeStruct((len(blocks_near),) + blocks_near[0].shape, BF16),
            [ANY] * (len(blocks_near) + len(order)),
            [pltpu.SemaphoreType.DMA((len(blocks_near),))],
            (*blocks_near, *order),
            megabytes=12 * scale,
        )
        return [joined, exchange(joined, "dp", 1)]

    notes_near = near(notes)
    direct = [chip for chip in range(1, owners // 2) if chip & (chip - 1) == 0]
    chip_groups = [[chip for chip in range(owners // 2) if chip not in direct], direct]
    g_pairs = []
    for group in chip_groups:
        g_pairs += over_core([g_near[chip] for chip in group], [notes])
    slopes, part, g_own = call(
        functools.partial(slopes_kernel, chip_groups, owners, heads, blocks, slots, tile_rows, in_place),
        [
            stack_shape,
            jax.ShapeDtypeStruct((slots, width + note_size, text_rows), BF16),
            jax.ShapeDtypeStruct((slots,) + g_near[0].shape, BF16),
        ],
        [SMEM] * 3 + [VMEM, stack_spec] + [VMEM] * 2 + [ANY] * len(g_pairs),
        [
            pltpu.VMEM((delta_rows, HEAD_DIM), F32),
            pltpu.SemaphoreType.DMA((slots,)),
        ],
        (*known, notes, weights, values, keys_turned, *g_pairs),
        out_specs=[stack_spec, VMEM, VMEM],
        grid=() if in_place else (slots * steps,),
        megabytes=20,
        cost=6,
    )
    notes_pair = over_core(notes_near, [part])
    factors = call(
        functools.partial(factors_kernel, owners, heads, groups, slots),
        jax.ShapeDtypeStruct((slots, heads, groups, HEAD_DIM), F32),
        [SMEM] * 3 + [VMEM] * 2,
        [pltpu.VMEM((owners, note_count, HEAD_DIM), BF16)],
        (*known, *notes_pair),
        cost=30,
    )
    kept, got = [], []

    def tile_sums(slot, order):
        left_spec = VMEM if in_place else pl.BlockSpec((1, padded, block_rows), lambda i: (slot * steps + i, 0, 0))
        keep, send = call(
            functools.partial(sums_kernel, owners, heads, blocks, slots, slot, in_place),
            [jax.ShapeDtypeStruct((padded, HEAD_DIM), BF16)] * 2,
            [SMEM] * 3 + [left_spec] * 2 + [VMEM] * 3 + [ANY] * len(order),
            [pltpu.VMEM((2, padded, HEAD_DIM), BF16 if in_place else F32)],
            (*known, weights, slopes, factors, q_own, g_own, *order),
            out_specs=[VMEM] * 2,
            grid=() if in_place else (steps,),
            megabytes=8 * scale,
            cost=4,
        )
        kept.append(keep)
        got.append(exchange(send, "seq", 1))

    tile_sums(0, [])
    routed = call(
        functools.partial(route_kernel, owners, heads, blocks, slots),
        [jax.ShapeDtypeStruct((width + note_size, text_rows), BF16)] * (owners // 2),
        [SMEM] * 3 + [VMEM] * 2 + [ANY] * 2,
        [],
        (*known, part, exchange(part, "dp", 1), factors, kept[0]),
        megabytes=14,
        cost=30,
    )

    for slot in range(1, slots):
        tile_sums(slot, [routed[0]])

    sums = [routed[0]] + [exchange(routed[d], "dp", 2 * d) for d in range(1, owners // 2)]
    cut = call(
        functools.partial(gather_kernel, heads, len(sums)),
        [jax.ShapeDtypeStruct((rows_dev, width), BF16)] * groups,
        [VMEM] * len(sums),
        [],
        sums,
        megabytes=8 * scale,
        cost=30,
    )
    back = [cut[0]] + [exchange(cut[j], "seq", j) for j in range(1, groups)]
    grad_tiles, merged = call(
        functools.partial(merge_kernel, slots),
        [jax.ShapeDtypeStruct((tile_rows, slots, HEAD_DIM), BF16), jax.ShapeDtypeStruct((TILE, HEAD_DIM), BF16)],
        [VMEM] * (2 * slots),
        [],
        (*kept, *got),
        cost=2,
    )
    grad_queries = call(
        place_kernel,
        jax.ShapeDtypeStruct((rows_dev, features), BF16),
        [SMEM] + [VMEM] * groups + [ANY],
        [],
        (who, *back, merged),
        cost=1,
    )
    return (grad_queries[None], jnp.transpose(grad_tiles, (1, 0, 2)))


def solution(mesh):
    placed = (
        P("dp", "seq", None),
        P("dp", "seq", None),
        P("dp", "seq", None),
        P("dp", None, "seq"),
        P(),
        P(),
        P("dp"),
    )
    return jax.shard_map(
        shards,
        mesh=mesh,
        in_specs=placed,
        out_specs=(P("dp", "seq", None), P("dp", None, "seq")),
        check_vma=False,
    )
```
